32 devices in a mesh: grp: 4 (over z), tile: 8 (over y, x, core).
Axes of the slice: x: 2, y: 2, z: 4, core: 2. Of those that a mesh axis runs over, the one named last changes fastest.
Arguments:
- embeddings: bfloat16 [12288, 1024], P(('grp', 'tile'))
- row_group: int32 [12288], P(('grp', 'tile')), may hold values from 0 to 3, as said below
- row_cluster: int32 [12288], P(('grp', 'tile')), may hold values from 0 to 1
Outputs:
- best_match: float32 [12288], P(('grp', 'tile'))
The draws below stay inside these ranges and needn't reach their ends.
Inputs may be any that keep to these rules, and one draw needn't show every extreme that they name: `row_group`: among the rows of one device no group is named by more than 192 rows; for every index along tile some group is named by exactly 192 rows on every device of that tile index.
All inputs are finite; a program needn't handle non-finite values.
Results may differ from the reference program's by a relative error of at most 0.00053.
Values may be sent and summed in bfloat16 or wider, within the bound.
A program may use at most 128 MiB of HBM per device.

```python
from functools import partial
import jax
import jax.numpy as jnp
from jax import lax

D = 1024
ROWS_DEV = 384
CL_GRP = 2
GROUPS = 4
TILES = 8
CAP = 192
ROWS = 12288


def assign_rows(key):
    key_busy, key_rank, key_order, key_cuts, key_cluster = jax.random.split(key, 5)
    block_count = GROUPS * TILES
    busiest = jnp.tile(jax.random.randint(key_busy, (TILES,), 0, GROUPS), GROUPS)
    ranking = jax.vmap(lambda single: jax.random.permutation(single, ROWS_DEV))(jax.random.split(key_rank, block_count))
    ordering = jax.vmap(lambda single: jax.random.permutation(single, GROUPS - 1))(jax.random.split(key_order, block_count))
    remaining = ROWS_DEV - CAP
    jitter = CAP // 8
    centres = jnp.arange(1, GROUPS - 1, dtype=jnp.int32) * remaining // (GROUPS - 1)
    cutoff = centres[None, :] + jax.random.randint(key_cuts, (block_count, GROUPS - 2), -jitter, jitter + 1)
    past_busy = ranking - CAP
    pieces = jnp.sum((past_busy[:, :, None] >= cutoff[:, None, :]).astype(jnp.int32), axis=2)
    others = (busiest[:, None] + 1 + jnp.take_along_axis(ordering, pieces, axis=1)) % GROUPS
    owners = jnp.where(ranking < CAP, busiest[:, None], others).reshape(ROWS).astype(jnp.int32)
    cluster = jax.random.randint(key_cluster, (ROWS,), 0, CL_GRP).astype(jnp.int32)
    return (owners, cluster)


def draw_row_group(key, part):
    owners, cluster = assign_rows(key)
    return owners


def draw_row_cluster(key, part):
    owners, cluster = assign_rows(key)
    return cluster


def draw_embeddings(key, part):
    owners, cluster = assign_rows(key)
    key = jax.random.fold_in(key, 11)
    key_noise, key_ties, key_mix = jax.random.split(key, 3)
    cluster_key = owners * CL_GRP + cluster
    tie_break = jax.random.permutation(key_ties, ROWS).astype(jnp.int32)
    sorting = jnp.argsort(cluster_key * ROWS + tie_break, stable=True).astype(jnp.int32)
    previous = jnp.concatenate([sorting[:1], sorting[:-1]])
    partner_sorted = jnp.where(cluster_key[previous] == cluster_key[sorting], previous, sorting)
    partner = jnp.zeros((ROWS,), jnp.int32).at[sorting].set(partner_sorted.astype(jnp.int32))
    mixing = jnp.exp(jax.random.uniform(key_mix, (ROWS, 1), jnp.float32, jnp.log(0.2), jnp.log(4.0)))
    base_noise = jnp.clip(jax.random.normal(key_noise, (ROWS, D), jnp.float32), -6.0, 6.0)
    values = base_noise + mixing * base_noise[partner]
    return values.astype(jnp.bfloat16)


def setup_inputs(seed: int = 0) -> dict:
    seeds = jax.random.split(jax.random.key(seed), 4)
    return {
        "embeddings": draw_embeddings(jax.random.fold_in(seeds[3], 71), 0),
        "row_group": draw_row_group(jax.random.fold_in(seeds[3], 71), 0),
        "row_cluster": draw_row_cluster(jax.random.fold_in(seeds[3], 71), 0),
    }


epsilon = 1e-06

def unit_rows(values):
    floats = values.astype(jnp.float32)
    scaled = floats * lax.rsqrt(lax.optimization_barrier(jnp.sum(floats * floats, axis=-1, keepdims=True)) + epsilon)
    return scaled.astype(jnp.bfloat16)

def slot_index(owners, groups, capacity):
    onehot = (owners[:, None] == jnp.arange(groups, dtype=jnp.int32)[None, :]).astype(jnp.int32)
    earlier = jnp.cumsum(onehot, axis=0) - onehot
    ranked = lax.optimization_barrier(jnp.sum(earlier * onehot, axis=1))
    return (owners * capacity + ranked).astype(jnp.int32)

def masked_table(scores, left_ids, right_ids, left_pos, right_pos):
    allowed = (left_ids[:, None] == right_ids[None, :]) & (right_ids[None, :] >= 0) & (left_pos[:, None] != right_pos[None, :])
    return jnp.where(allowed, scores, jnp.float32(-1.0))

def fill_slots(normed, where_to, cluster_tags):
    buffer = jnp.zeros((GROUPS * CAP, D), jnp.bfloat16).at[where_to].set(normed)
    tagged = jnp.full((GROUPS * CAP,), -1, jnp.int32).at[where_to].set(cluster_tags)
    return (buffer, tagged)

def reference(embeddings, row_group, row_cluster):
    blocks = GROUPS * TILES
    slots_all = GROUPS * CAP
    normed = unit_rows(embeddings).reshape(blocks, ROWS_DEV, D)
    owners = row_group.reshape(blocks, ROWS_DEV)
    labels = row_cluster.reshape(blocks, ROWS_DEV)
    placed = jax.vmap(partial(slot_index, groups=GROUPS, capacity=CAP))(owners)
    buffers, tagged = jax.vmap(fill_slots)(normed, placed, labels)
    buffers = buffers.reshape(GROUPS, TILES, GROUPS, CAP, D).transpose(2, 1, 0, 3, 4).reshape(GROUPS, TILES * slots_all, D)
    tagged = tagged.reshape(GROUPS, TILES, GROUPS, CAP).transpose(2, 1, 0, 3).reshape(GROUPS, TILES * slots_all)
    positions = jnp.arange(TILES * slots_all, dtype=jnp.int32)

    def per_group(operands):
        members, member_ids = operands
        floats = members.astype(jnp.float32)

        def per_tile(tile_index):
            first_row = (tile_index * slots_all).astype(jnp.int32)
            queries = lax.dynamic_slice_in_dim(floats, first_row, slots_all, 0)
            query_ids = lax.dynamic_slice_in_dim(member_ids, first_row, slots_all, 0)
            query_pos = first_row + jnp.arange(slots_all, dtype=jnp.int32)
            scores = jnp.dot(queries, floats.T, precision=lax.Precision.HIGHEST)
            return lax.optimization_barrier(jnp.max(masked_table(scores, query_ids, member_ids, query_pos, positions), axis=1))
        return lax.map(per_tile, jnp.arange(TILES, dtype=jnp.int32))
    results = lax.map(per_group, (buffers, tagged))
    results = results.reshape(GROUPS, TILES, GROUPS, CAP).transpose(2, 1, 0, 3).reshape(blocks, slots_all)
    return jnp.take_along_axis(results, placed, axis=1).reshape(ROWS)
```

```python
import functools

import jax
import jax.numpy as jnp
from jax import lax
from jax.experimental import pallas as pl
from jax.experimental.pallas import tpu as pltpu
from jax.sharding import PartitionSpec as P

MESH = pl.DeviceIdType.MESH
epsilon = 1e-06
NT = (((1,), (1,)), ((), ()))


def unit_rows(values):
    floats = values.astype(jnp.float32)
    scaled = floats * lax.rsqrt(jnp.sum(floats * floats, axis=-1, keepdims=True) + epsilon)
    return scaled.astype(jnp.bfloat16)


def slot_index(owners, groups, capacity):
    onehot = (owners[:, None] == jnp.arange(groups, dtype=jnp.int32)[None, :]).astype(jnp.int32)
    earlier = jnp.cumsum(onehot, axis=0) - onehot
    ranked = jnp.sum(earlier * onehot, axis=1)
    return owners * capacity + ranked


def masked_table(scores, left_ids, right_ids, left_pos, right_pos):
    allowed = (
        (left_ids[:, None] == right_ids[None, :])
        & (right_ids[None, :] >= 0)
        & (left_pos[:, None] != right_pos[None, :])
    )
    return jnp.where(allowed, scores, jnp.float32(-1.0))


def local_general(embeddings, row_group, row_cluster):
    row_count = embeddings.shape[0]
    columns = embeddings.shape[1]
    groups = lax.axis_size("grp")
    capacity = 2 * row_count // groups
    slots_all = groups * capacity
    placed = slot_index(row_group, groups, capacity)
    normed = unit_rows(embeddings)
    outgoing = (
        jnp.zeros((slots_all, columns), jnp.bfloat16)
        .at[placed]
        .set(normed)
        .reshape(groups, capacity, columns)
    )
    out_tags = (
        jnp.full((slots_all,), -1, jnp.int32).at[placed].set(row_cluster).reshape(groups, capacity)
    )
    members, member_ids = (
        lax.all_to_all(outgoing, "grp", split_axis=0, concat_axis=0, tiled=True),
        lax.all_to_all(out_tags, "grp", split_axis=0, concat_axis=0, tiled=True),
    )
    members = members.reshape(slots_all, columns)
    member_ids = member_ids.reshape(slots_all)
    tile_here = lax.axis_index("tile")
    local_pos = jnp.arange(slots_all, dtype=jnp.int32)
    own_pos = tile_here * slots_all + local_pos
    start_best = jnp.full((slots_all,), -1.0, jnp.float32)
    piece_rows = lax.all_gather(members, "tile", axis=0, tiled=True)
    piece_ids = lax.all_gather(member_ids, "tile", axis=0, tiled=True)
    scores = jnp.einsum("id,jd->ij", members, piece_rows, preferred_element_type=jnp.float32)
    piece_pos = jnp.arange(piece_rows.shape[0], dtype=jnp.int32)
    best_sim = jnp.maximum(
        start_best, jnp.max(masked_table(scores, member_ids, piece_ids, own_pos, piece_pos), axis=1)
    )
    results = best_sim.reshape(groups, capacity)
    arrived = lax.all_to_all(results, "grp", split_axis=0, concat_axis=0, tiled=True)
    return jnp.take(arrived.reshape(slots_all), placed)


def kernel(
    x_ref, owner_ref, cluster_ref, out_ref,
    normed, send, queries, keys, tag_out, tag_in, tag_own, tag_far, best, result_in,
    ztag_s, ztag_r, z_s, z_r, ftag_s, ftag_r, sib_s, sib_r, near_s, near_r, relay_s, relay_r, res_s, res_r,
):
    rows = x_ref.shape[0]
    groups = 4
    cap = 2 * rows // groups
    slots = groups * cap
    half = cap // 2
    me = lax.axis_index("grp")
    tile = lax.axis_index("tile")
    core = lax.rem(tile, 2)
    xpos = lax.rem(tile // 2, 2)
    ypos = tile // 4
    sib = tile + 1 - 2 * core
    xstep = 2 - 4 * xpos
    ystep = 4 - 8 * ypos
    near = (tile + xstep, tile + ystep)
    far = tile + xstep + ystep

    def other(r):
        return lax.rem(me + r, groups)

    partners = [(other(r), tile) for r in (1, 2, 3)]
    partners += [(other(r), sib) for r in (0, 1, 2, 3)]
    partners += [(me, near[0]), (me, near[1]), (me, far)]
    barrier = pltpu.get_barrier_semaphore()
    for partner in partners:
        pl.semaphore_signal(barrier, inc=1, device_id=partner, device_id_type=MESH)

    def remote(src, dst, ssem, rsem, device):
        return pltpu.make_async_remote_copy(
            src_ref=src, dst_ref=dst, send_sem=ssem, recv_sem=rsem, device_id=device, device_id_type=MESH
        )

    owner = owner_ref[...]
    cluster = cluster_ref[...]
    group_of = lax.broadcasted_iota(jnp.int32, (8, rows), 0)
    belongs = group_of == owner
    before = lax.broadcasted_iota(jnp.int32, (rows, rows), 0) < lax.broadcasted_iota(jnp.int32, (rows, rows), 1)
    earlier = jnp.dot(
        jnp.where(belongs, 1.0, 0.0).astype(jnp.bfloat16),
        jnp.where(before, 1.0, 0.0).astype(jnp.bfloat16),
        preferred_element_type=jnp.float32,
    )
    rank = jnp.sum(jnp.where(belongs, earlier, 0.0), axis=0, keepdims=True).astype(jnp.int32)
    slot = owner * cap + rank
    place = me * cap + rank
    at_place = jnp.where(lax.broadcasted_iota(jnp.int32, (slots, rows), 0) == place, 1.0, 0.0).astype(jnp.bfloat16)

    marks = jnp.where(belongs, (cluster + 1).astype(jnp.float32), 0.0).astype(jnp.bfloat16)
    tag_out[...] = lax.dot_general(marks, at_place, NT, preferred_element_type=jnp.float32)

    chunk = rows // 4
    for c in range(4):
        part = pl.ds(c * chunk, chunk)
        normed[part, :] = unit_rows(x_ref[part, :])

    pl.semaphore_wait(barrier, len(partners))

    ztags = []
    for r in (1, 2, 3):
        copy = remote(tag_out, tag_in.at[r - 1], ztag_s.at[r - 1], ztag_r.at[r - 1], (other(groups - r), tile))
        copy.start()
        ztags.append(copy)

    def filled(group):
        sel = lax.broadcasted_iota(jnp.int32, (cap, rows), 0) + group * cap
        sel = jnp.where(sel == slot, 1.0, 0.0).astype(jnp.bfloat16)
        return jnp.dot(sel, normed[...], preferred_element_type=jnp.float32).astype(jnp.bfloat16)

    def piece(r):
        return pl.ds(pl.multiple_of(other(r) * cap, cap), cap)

    zcopies = {}
    for r in (2, 3, 1):
        send[r - 1] = filled(other(groups - r))
        copy = remote(
            send.at[r - 1], queries.at[piece(0), :], z_s.at[r - 1], z_r.at[r - 1], (other(groups - r), tile)
        )
        copy.start()
        zcopies[r] = copy
    queries[piece(0), :] = filled(me)

    pending = []

    def arrival(r):
        return remote(send.at[r - 1], queries.at[piece(r), :], z_s.at[r - 1], z_r.at[r - 1], (other(groups - r), tile))

    def spread(i, r):
        src = queries.at[piece(r), :]
        copies = [
            remote(src, queries.at[pl.ds(pl.multiple_of(slots + other(r) * cap, cap), cap), :],
                   sib_s.at[i], sib_r.at[i], (me, sib)),
            remote(src, keys.at[0, piece(r), :], near_s.at[0, i], near_r.at[0, i], (me, near[0])),
            remote(src, keys.at[1, piece(r), :], near_s.at[1, i], near_r.at[1, i], (me, near[1])),
        ]
        for copy in copies[::-1]:
            copy.start()
        return copies

    def relay(i, r, copies):
        made = []
        for n in (0, 1):
            copies[1 + n].wait_recv()
            lines = pl.ds(pl.multiple_of(other(r) * cap + n * half, half), half)
            copy = remote(keys.at[n, lines, :], keys.at[2, lines, :], relay_s.at[n, i], relay_r.at[n, i], (me, near[1 - n]))
            copy.start()
            made.append(copy)
        return made

    order = (0, 1, 3, 2)
    spreads, relays = [spread(0, 0)], []

    for copy in ztags:
        copy.wait_recv()
    total = tag_out[...] + tag_in[0] + tag_in[1] + tag_in[2]
    mine = jnp.sum(jnp.where(lax.broadcasted_iota(jnp.int32, (8, slots), 0) == me, total, 0.0), axis=0, keepdims=True)
    tag_own[...] = jnp.broadcast_to(mine, (8, slots))
    ftags = []
    for n, device in enumerate((sib, near[0], near[1], far)):
        copy = remote(tag_own, tag_far.at[n], ftag_s.at[n], ftag_r.at[n], (me, device))
        copy.start()
        ftags.append(copy)

    for i in (1, 2, 3):
        zcopies[order[i]].wait_recv()
        spreads.append(spread(i, order[i]))
        relays.append(relay(i - 1, order[i - 1], spreads[i - 1]))

    for copy in ftags:
        copy.wait_recv()
    for copies in spreads:
        copies[0].wait_recv()

    best[...] = jnp.full(best.shape, -1.0, jnp.float32)

    def compare(keys_at, key_tags, own_first):
        lines = keys_at[...]
        for h in (0, 1):
            scores = lax.dot_general(
                lines, queries[h * slots : (h + 1) * slots, :], NT, preferred_element_type=jnp.float32
            )
            query_tags = tag_own[0:1, :] if h == 0 else tag_far[0, 0:1, :]
            allowed = key_tags == query_tags
            if h == 0 and own_first is not None:
                row_at = lax.broadcasted_iota(jnp.int32, (cap, slots), 0) + own_first
                allowed = allowed & (row_at != lax.broadcasted_iota(jnp.int32, (cap, slots), 1))
            found = jnp.max(jnp.where(allowed, scores, -1.0), axis=0, keepdims=True)
            best[h] = jnp.maximum(best[h], found)

    def column(tags, r):
        lanes = lax.broadcasted_iota(jnp.int32, (cap, slots), 1)
        wanted = lax.broadcasted_iota(jnp.int32, (cap, slots), 0) + other(r) * cap
        picked = jnp.sum(jnp.where(lanes == wanted, tags, 0.0), axis=1, keepdims=True)
        return jnp.where(picked > 0.0, picked, -1.0)

    def step(i):
        return lax.select(i < 2, i, 5 - i)

    @pl.loop(0, 4)
    def _(i):
        r = step(i)
        compare(queries.at[piece(r), :], column(tag_own[0:1, :], r), other(r) * cap)

    relays.append(relay(3, order[3], spreads[3]))

    for n in (0, 1):
        @pl.loop(0, 4)
        def _(i):
            r = step(i)
            compare(keys.at[n, piece(r), :], column(tag_far[1 + n, 0:1, :], r), None)

    for i in range(4):
        for copy in relays[i]:
            copy.wait_recv()
        r = order[i]
        compare(keys.at[2, piece(r), :], column(tag_far[3, 0:1, :], r), None)

    copies = []
    for h, device in enumerate((tile, sib)):
        for r in range(4):
            index = h * 4 + r
            if index == 0:
                result_in[0] = best[0]
                continue
            copy = remote(best.at[h], result_in.at[index], res_s.at[index], res_r.at[index], (other(groups - r), device))
            copy.start()
            copies.append(copy)
    for copy in copies:
        copy.wait_recv()

    out = jnp.zeros((1, rows), jnp.float32)
    for r in range(4):
        block = jnp.maximum(result_in[r], result_in[4 + r])
        high = block.astype(jnp.bfloat16)
        rest = block - high.astype(jnp.float32)
        middle = rest.astype(jnp.bfloat16)
        low = (rest - middle.astype(jnp.float32)).astype(jnp.bfloat16)
        picked = [
            jnp.dot(term, at_place, preferred_element_type=jnp.float32)[0:1, :] for term in (high, middle, low)
        ]
        value = (picked[0] + picked[1]) + picked[2]
        out = jnp.where(owner == other(r), value, out)
    out_ref[...] = out

    for copy in ztags + ftags + copies + list(zcopies.values()):
        copy.wait_send()
    for group in spreads + relays:
        for copy in group:
            copy.wait_send()


def local_fused(embeddings, row_group, row_cluster):
    rows, columns = embeddings.shape
    slots = 2 * rows
    dma = pltpu.SemaphoreType.DMA
    out = pl.pallas_call(
        kernel,
        out_shape=jax.ShapeDtypeStruct((1, rows), jnp.float32),
        in_specs=[pl.BlockSpec(memory_space=pltpu.VMEM)] * 3,
        out_specs=pl.BlockSpec(memory_space=pltpu.VMEM),
        scratch_shapes=[
            pltpu.VMEM((rows, columns), jnp.bfloat16),
            pltpu.VMEM((3, slots // 4, columns), jnp.bfloat16),
            pltpu.VMEM((2 * slots, columns), jnp.bfloat16),
            pltpu.VMEM((3, slots, columns), jnp.bfloat16),
            pltpu.VMEM((8, slots), jnp.float32),
            pltpu.VMEM((3, 8, slots), jnp.float32),
            pltpu.VMEM((8, slots), jnp.float32),
            pltpu.VMEM((4, 8, slots), jnp.float32),
            pltpu.VMEM((2, 8, slots), jnp.float32),
            pltpu.VMEM((8, 8, slots), jnp.float32),
            dma((3,)), dma((3,)), dma((3,)), dma((3,)),
            dma((4,)), dma((4,)), dma((4,)), dma((4,)),
            dma((2, 4)), dma((2, 4)), dma((2, 4)), dma((2, 4)),
            dma((8,)), dma((8,)),
        ],
        compiler_params=pltpu.CompilerParams(
            collective_id=0, has_side_effects=True, vmem_limit_bytes=48 * 1024 * 1024
        ),
    )(embeddings, row_group.reshape(1, rows), row_cluster.reshape(1, rows))
    return out.reshape(rows)


def solution(mesh):
    fused = mesh.shape["grp"] == 4 and mesh.shape["tile"] == 8
    placed = (P(("grp", "tile"), None), P(("grp", "tile")), P(("grp", "tile")))
    return jax.shard_map(
        local_fused if fused else local_general,
        mesh=mesh, in_specs=placed, out_specs=P(("grp", "tile")), check_vma=False,
    )
```

```python
import jax
import jax.numpy as jnp
from jax import lax
from jax.experimental import pallas as pl
from jax.experimental.pallas import tpu as pltpu
from jax.sharding import PartitionSpec as P

MESH = pl.DeviceIdType.MESH
epsilon = 1e-06
NT = (((1,), (1,)), ((), ()))


def unit_rows(values):
    floats = values.astype(jnp.float32)
    scaled = floats * lax.rsqrt(jnp.sum(floats * floats, axis=-1, keepdims=True) + epsilon)
    return scaled.astype(jnp.bfloat16)


def slot_index(owners, groups, capacity):
    onehot = (owners[:, None] == jnp.arange(groups, dtype=jnp.int32)[None, :]).astype(jnp.int32)
    earlier = jnp.cumsum(onehot, axis=0) - onehot
    ranked = jnp.sum(earlier * onehot, axis=1)
    return owners * capacity + ranked


def masked_table(scores, left_ids, right_ids, left_pos, right_pos):
    allowed = (
        (left_ids[:, None] == right_ids[None, :])
        & (right_ids[None, :] >= 0)
        & (left_pos[:, None] != right_pos[None, :])
    )
    return jnp.where(allowed, scores, jnp.float32(-1.0))


def local_general(embeddings, row_group, row_cluster):
    row_count = embeddings.shape[0]
    columns = embeddings.shape[1]
    groups = lax.axis_size("grp")
    capacity = 2 * row_count // groups
    slots_all = groups * capacity
    placed = slot_index(row_group, groups, capacity)
    normed = unit_rows(embeddings)
    outgoing = (
        jnp.zeros((slots_all, columns), jnp.bfloat16)
        .at[placed]
        .set(normed)
        .reshape(groups, capacity, columns)
    )
    out_tags = (
        jnp.full((slots_all,), -1, jnp.int32).at[placed].set(row_cluster).reshape(groups, capacity)
    )
    members, member_ids = (
        lax.all_to_all(outgoing, "grp", split_axis=0, concat_axis=0, tiled=True),
        lax.all_to_all(out_tags, "grp", split_axis=0, concat_axis=0, tiled=True),
    )
    members = members.reshape(slots_all, columns)
    member_ids = member_ids.reshape(slots_all)
    tile_here = lax.axis_index("tile")
    local_pos = jnp.arange(slots_all, dtype=jnp.int32)
    own_pos = tile_here * slots_all + local_pos
    start_best = jnp.full((slots_all,), -1.0, jnp.float32)
    piece_rows = lax.all_gather(members, "tile", axis=0, tiled=True)
    piece_ids = lax.all_gather(member_ids, "tile", axis=0, tiled=True)
    scores = jnp.einsum("id,jd->ij", members, piece_rows, preferred_element_type=jnp.float32)
    piece_pos = jnp.arange(piece_rows.shape[0], dtype=jnp.int32)
    best_sim = jnp.maximum(
        start_best, jnp.max(masked_table(scores, member_ids, piece_ids, own_pos, piece_pos), axis=1)
    )
    results = best_sim.reshape(groups, capacity)
    arrived = lax.all_to_all(results, "grp", split_axis=0, concat_axis=0, tiled=True)
    return jnp.take(arrived.reshape(slots_all), placed)


def kernel(
    x_ref, owner_ref, cluster_ref, out_ref,
    normed, send, queries, keys, tag_out, tag_in, tag_own, tag_far, query_tags, key_tags, best, result_out, result_in,
    ztag_s, ztag_r, z_s, z_r, ftag_s, ftag_r, sib_s, sib_r, near_s, near_r, relay_s, relay_r, res_s, res_r,
):
    rows = x_ref.shape[0]
    groups = 4
    cap = 2 * rows // groups
    slots = groups * cap
    half = cap // 2
    width = query_tags.shape[2]
    me = lax.axis_index("grp")
    tile = lax.axis_index("tile")
    core = lax.rem(tile, 2)
    xpos = lax.rem(tile // 2, 2)
    ypos = tile // 4
    sib = tile + 1 - 2 * core
    xstep = 2 - 4 * xpos
    ystep = 4 - 8 * ypos
    near = (tile + xstep, tile + ystep)
    far = tile + xstep + ystep
    peer = (me, me + 1 - 2 * lax.rem(me, 2), me + 2 - 4 * (me // 2), 3 - me)

    partners = [(peer[r], tile) for r in (1, 2, 3)]
    partners += [(peer[r], sib) for r in (0, 1, 2, 3)]
    partners += [(me, near[0]), (me, near[1]), (me, far)]
    barrier = pltpu.get_barrier_semaphore()
    for partner in partners:
        pl.semaphore_signal(barrier, inc=1, device_id=partner, device_id_type=MESH)

    def remote(src, dst, ssem, rsem, device):
        return pltpu.make_async_remote_copy(
            src_ref=src, dst_ref=dst, send_sem=ssem, recv_sem=rsem, device_id=device, device_id_type=MESH
        )

    owner = owner_ref[...]
    cluster = cluster_ref[...]
    group_of = lax.broadcasted_iota(jnp.int32, (8, rows), 0)
    belongs = group_of == owner
    before = lax.broadcasted_iota(jnp.int32, (rows, rows), 0) < lax.broadcasted_iota(jnp.int32, (rows, rows), 1)
    earlier = jnp.dot(
        jnp.where(belongs, 1.0, 0.0).astype(jnp.bfloat16),
        jnp.where(before, 1.0, 0.0).astype(jnp.bfloat16),
        preferred_element_type=jnp.float32,
    )
    rank = jnp.sum(jnp.where(belongs, earlier, 0.0), axis=0, keepdims=True).astype(jnp.int32)
    slot = owner * cap + rank
    place = me * cap + rank
    at_place = jnp.where(lax.broadcasted_iota(jnp.int32, (slots, rows), 0) == place, 1.0, 0.0).astype(jnp.bfloat16)

    marks = jnp.where(belongs, (cluster + 1).astype(jnp.float32), 0.0).astype(jnp.bfloat16)
    tag_out[...] = lax.dot_general(marks, at_place, NT, preferred_element_type=jnp.float32)

    chunk = rows // 4
    for c in range(4):
        part = pl.ds(c * chunk, chunk)
        normed[part, :] = unit_rows(x_ref[part, :])

    pl.semaphore_wait(barrier, len(partners))

    ztags = []
    for r in (1, 2, 3):
        copy = remote(tag_out, tag_in.at[r - 1], ztag_s.at[r - 1], ztag_r.at[r - 1], (peer[r], tile))
        copy.start()
        ztags.append(copy)

    def filled(group):
        sel = lax.broadcasted_iota(jnp.int32, (cap, rows), 0) + group * cap
        sel = jnp.where(sel == slot, 1.0, 0.0).astype(jnp.bfloat16)
        return jnp.dot(sel, normed[...], preferred_element_type=jnp.float32).astype(jnp.bfloat16)

    def piece(r):
        return pl.ds(pl.multiple_of(peer[r] * cap, cap), cap)

    def zcopy(r):
        return remote(send.at[r - 1], queries.at[piece(0), :], z_s.at[r - 1], z_r.at[r - 1], (peer[r], tile))

    def spread(i):
        src = queries.at[piece(i), :]
        beside = pl.ds(pl.multiple_of(slots + peer[i] * cap, cap), cap)
        line = pl.ds(i * cap, cap)
        copies = [
            remote(src, queries.at[beside, :], sib_s.at[i], sib_r.at[i], (me, sib)),
            remote(src, keys.at[0, line, :], near_s.at[0, i], near_r.at[0, i], (me, near[0])),
            remote(src, keys.at[1, line, :], near_s.at[1, i], near_r.at[1, i], (me, near[1])),
        ]
        for copy in copies[::-1]:
            copy.start()
        return copies

    def relay(i, copies):
        made = []
        for n in (0, 1):
            copies[1 + n].wait_recv()
            line = pl.ds(i * cap + n * half, half)
            copy = remote(keys.at[n, line, :], keys.at[2, line, :], relay_s.at[n, i], relay_r.at[n, i], (me, near[1 - n]))
            copy.start()
            made.append(copy)
        return made

    zcopies = {}
    for r in (2, 1):
        send[r - 1] = filled(peer[r])
        zcopies[r] = zcopy(r)
        zcopies[r].start()
    queries[piece(0), :] = filled(me)
    spreads, relays = [spread(0)], []
    send[2] = filled(peer[3])

    for copy in ztags:
        copy.wait_recv()
    total = tag_out[...] + tag_in[0] + tag_in[1] + tag_in[2]
    mine = jnp.sum(jnp.where(lax.broadcasted_iota(jnp.int32, (8, slots), 0) == me, total, 0.0), axis=0, keepdims=True)
    tag_own[...] = jnp.broadcast_to(mine, (8, slots))
    ftags = []
    for n, device in enumerate((sib, near[0], near[1], far)):
        copy = remote(tag_own, tag_far.at[n], ftag_s.at[n], ftag_r.at[n], (me, device))
        copy.start()
        ftags.append(copy)

    relays.append(relay(0, spreads[0]))
    zcopies[2].wait_send()
    zcopies[3] = zcopy(3)
    zcopies[3].start()
    zcopies[1].wait_recv()
    spreads.append(spread(1))
    zcopies[2].wait_recv()
    spreads.append(spread(2))

    def column(tags, sources, n):
        for i in range(groups):
            lanes = lax.broadcasted_iota(jnp.int32, (cap, slots), 1)
            wanted = lax.broadcasted_iota(jnp.int32, (cap, slots), 0) + sources[i] * cap
            picked = jnp.sum(jnp.where(lanes == wanted, tags, 0.0), axis=1, keepdims=True)
            picked = jnp.where(picked > 0.0, picked, -1.0)
            key_tags[n, i * cap : (i + 1) * cap, :] = jnp.broadcast_to(picked, (cap, 128))

    for copy in ftags:
        copy.wait_recv()
    for c in range(slots // width):
        query_tags[c] = tag_own[:, c * width : (c + 1) * width]
        query_tags[slots // width + c] = tag_far[0, :, c * width : (c + 1) * width]
    column(tag_own[0:1, :], range(groups), 3)
    for n in (0, 1, 2):
        column(tag_far[1 + n, 0:1, :], peer, n)
    best[...] = jnp.full(best.shape, -1.0, jnp.float32)

    relays.append(relay(1, spreads[1]))
    relays.append(relay(2, spreads[2]))
    zcopies[3].wait_recv()
    spreads.append(spread(3))
    for copies in spreads:
        copies[0].wait_recv()

    def compare(source, n, first, count, own):
        @pl.loop(0, 2 * slots // width)
        def _(c):
            asked = queries[pl.ds(pl.multiple_of(c * width, width), width), :]
            scores = lax.dot_general(source[...], asked, NT, preferred_element_type=jnp.float32)
            tags = key_tags[n, first : first + count, :]
            allowed = jnp.concatenate([tags] * (width // 128), axis=1) == query_tags[c, 0:1, :]
            if own:
                line = lax.broadcasted_iota(jnp.int32, (count, width), 0)
                lane = lax.broadcasted_iota(jnp.int32, (count, width), 1) + c * width
                allowed = allowed & (line != lane)
            found = jnp.max(jnp.where(allowed, scores, -1.0), axis=0, keepdims=True)
            best[c] = jnp.maximum(best[c], found)

    def key_part(n, first, last):
        compare(keys.at[n, first * cap : last * cap, :], n, first * cap, (last - first) * cap, False)

    compare(queries.at[0:slots, :], 3, 0, slots, True)
    key_part(0, 0, 3)
    key_part(1, 0, 3)
    relays.append(relay(3, spreads[3]))
    for made in relays[:3]:
        for copy in made:
            copy.wait_recv()
    key_part(2, 0, 3)
    key_part(0, 3, 4)
    key_part(1, 3, 4)
    for copy in relays[3]:
        copy.wait_recv()
    key_part(2, 3, 4)

    for h in (0, 1):
        for c in range(slots // width):
            result_out[h, :, c * width : (c + 1) * width] = best[h * (slots // width) + c]
    copies = []
    for h, device in enumerate((tile, sib)):
        for r in range(4):
            index = h * 4 + r
            if index == 0:
                result_in[0] = result_out[0]
                continue
            copy = remote(
                result_out.at[h], result_in.at[index], res_s.at[index], res_r.at[index], (peer[r], device)
            )
            copy.start()
            copies.append(copy)
    for copy in copies:
        copy.wait_recv()

    out = jnp.zeros((1, rows), jnp.float32)
    for r in range(4):
        block = jnp.maximum(result_in[r], result_in[4 + r])
        high = block.astype(jnp.bfloat16)
        rest = block - high.astype(jnp.float32)
        middle = rest.astype(jnp.bfloat16)
        low = (rest - middle.astype(jnp.float32)).astype(jnp.bfloat16)
        picked = [
            jnp.dot(term, at_place, preferred_element_type=jnp.float32)[0:1, :] for term in (high, middle, low)
        ]
        value = (picked[0] + picked[1]) + picked[2]
        out = jnp.where(owner == peer[r], value, out)
    out_ref[...] = out

    for copy in ztags + ftags + copies + [zcopies[1], zcopies[3]]:
        copy.wait_send()
    for group in spreads + relays:
        for copy in group:
            copy.wait_send()


def local_fused(embeddings, row_group, row_cluster):
    rows, columns = embeddings.shape
    slots = 2 * rows
    width = 256
    dma = pltpu.SemaphoreType.DMA
    out = pl.pallas_call(
        kernel,
        out_shape=jax.ShapeDtypeStruct((1, rows), jnp.float32),
        in_specs=[pl.BlockSpec(memory_space=pltpu.VMEM)] * 3,
        out_specs=pl.BlockSpec(memory_space=pltpu.VMEM),
        scratch_shapes=[
            pltpu.VMEM((rows, columns), jnp.bfloat16),
            pltpu.VMEM((3, slots // 4, columns), jnp.bfloat16),
            pltpu.VMEM((2 * slots, columns), jnp.bfloat16),
            pltpu.VMEM((3, slots, columns), jnp.bfloat16),
            pltpu.VMEM((8, slots), jnp.float32),
            pltpu.VMEM((3, 8, slots), jnp.float32),
            pltpu.VMEM((8, slots), jnp.float32),
            pltpu.VMEM((4, 8, slots), jnp.float32),
            pltpu.VMEM((2 * slots // width, 8, width), jnp.float32),
            pltpu.VMEM((4, slots, 128), jnp.float32),
            pltpu.VMEM((2 * slots // width, 8, width), jnp.float32),
            pltpu.VMEM((2, 8, slots), jnp.float32),
            pltpu.VMEM((8, 8, slots), jnp.float32),
            dma((3,)), dma((3,)), dma((3,)), dma((3,)),
            dma((4,)), dma((4,)), dma((4,)), dma((4,)),
            dma((2, 4)), dma((2, 4)), dma((2, 4)), dma((2, 4)),
            dma((8,)), dma((8,)),
        ],
        compiler_params=pltpu.CompilerParams(
            collective_id=0, has_side_effects=True, vmem_limit_bytes=48 * 1024 * 1024
        ),
    )(embeddings, row_group.reshape(1, rows), row_cluster.reshape(1, rows))
    return out.reshape(rows)


def solution(mesh):
    fused = mesh.shape["grp"] == 4 and mesh.shape["tile"] == 8
    placed = (P(("grp", "tile"), None), P(("grp", "tile")), P(("grp", "tile")))
    return jax.shard_map(
        local_fused if fused else local_general,
        mesh=mesh, in_specs=placed, out_specs=P(("grp", "tile")), check_vma=False,
    )
```

```python
import jax
import jax.numpy as jnp
from jax import lax
from jax.experimental import pallas as pl
from jax.experimental.pallas import tpu as pltpu
from jax.sharding import PartitionSpec as P

MESH = pl.DeviceIdType.MESH
epsilon = 1e-06
NT = (((1,), (1,)), ((), ()))


def unit_rows(values):
    floats = values.astype(jnp.float32)
    scaled = floats * lax.rsqrt(jnp.sum(floats * floats, axis=-1, keepdims=True) + epsilon)
    return scaled.astype(jnp.bfloat16)


def slot_index(owners, groups, capacity):
    onehot = (owners[:, None] == jnp.arange(groups, dtype=jnp.int32)[None, :]).astype(jnp.int32)
    earlier = jnp.cumsum(onehot, axis=0) - onehot
    ranked = jnp.sum(earlier * onehot, axis=1)
    return owners * capacity + ranked


def masked_table(scores, left_ids, right_ids, left_pos, right_pos):
    allowed = (
        (left_ids[:, None] == right_ids[None, :])
        & (right_ids[None, :] >= 0)
        & (left_pos[:, None] != right_pos[None, :])
    )
    return jnp.where(allowed, scores, jnp.float32(-1.0))


def local_general(embeddings, row_group, row_cluster):
    row_count = embeddings.shape[0]
    columns = embeddings.shape[1]
    groups = lax.axis_size("grp")
    capacity = 2 * row_count // groups
    slots_all = groups * capacity
    placed = slot_index(row_group, groups, capacity)
    normed = unit_rows(embeddings)
    outgoing = (
        jnp.zeros((slots_all, columns), jnp.bfloat16)
        .at[placed]
        .set(normed)
        .reshape(groups, capacity, columns)
    )
    out_tags = (
        jnp.full((slots_all,), -1, jnp.int32).at[placed].set(row_cluster).reshape(groups, capacity)
    )
    members, member_ids = (
        lax.all_to_all(outgoing, "grp", split_axis=0, concat_axis=0, tiled=True),
        lax.all_to_all(out_tags, "grp", split_axis=0, concat_axis=0, tiled=True),
    )
    members = members.reshape(slots_all, columns)
    member_ids = member_ids.reshape(slots_all)
    tile_here = lax.axis_index("tile")
    local_pos = jnp.arange(slots_all, dtype=jnp.int32)
    own_pos = tile_here * slots_all + local_pos
    start_best = jnp.full((slots_all,), -1.0, jnp.float32)
    piece_rows = lax.all_gather(members, "tile", axis=0, tiled=True)
    piece_ids = lax.all_gather(member_ids, "tile", axis=0, tiled=True)
    scores = jnp.einsum("id,jd->ij", members, piece_rows, preferred_element_type=jnp.float32)
    piece_pos = jnp.arange(piece_rows.shape[0], dtype=jnp.int32)
    best_sim = jnp.maximum(
        start_best, jnp.max(masked_table(scores, member_ids, piece_ids, own_pos, piece_pos), axis=1)
    )
    results = best_sim.reshape(groups, capacity)
    arrived = lax.all_to_all(results, "grp", split_axis=0, concat_axis=0, tiled=True)
    return jnp.take(arrived.reshape(slots_all), placed)


def kernel(
    x_ref, owner_ref, cluster_ref, out_ref,
    normed, send, members, tag_out, tag_in, tags, query_tags, key_tags, best, result_out, result_in, picks,
    ztag_s, ztag_r, z_s, z_r, ptag_s, ptag_r, sib_s, sib_r, near_s, near_r, relay_s, relay_r, res_s, res_r,
):
    rows = x_ref.shape[0]
    groups = 4
    cap = 2 * rows // groups
    slots = groups * cap
    half = slots // 2
    me = lax.axis_index("grp")
    tile = lax.axis_index("tile")
    core = lax.rem(tile, 2)
    xpos = lax.rem(tile // 2, 2)
    ypos = tile // 4
    beside = 1 - 2 * core
    sib = tile + beside
    xdev = tile + 2 - 4 * xpos
    ydev = tile + 4 - 8 * ypos
    cross = 4 - xpos
    crossdev = ydev + (1 - xpos) * beside
    peer = (me, me + 1 - 2 * lax.rem(me, 2), me + 2 - 4 * (me // 2), 3 - me)
    early = me // 2
    late = 1 - early

    partners = [(peer[r], tile) for r in (1, 2, 3)]
    partners += [(peer[r], device) for r in range(4) for device in (sib, xdev, ydev, ydev + beside)]
    barrier = pltpu.get_barrier_semaphore()
    for partner in partners:
        pl.semaphore_signal(barrier, inc=1, device_id=partner, device_id_type=MESH)

    def remote(src, dst, ssem, rsem, device):
        return pltpu.make_async_remote_copy(
            src_ref=src, dst_ref=dst, send_sem=ssem, recv_sem=rsem, device_id=device, device_id_type=MESH
        )

    owner = owner_ref[...]
    cluster = cluster_ref[...]
    group_of = lax.broadcasted_iota(jnp.int32, (8, rows), 0)
    belongs = group_of == owner
    before = lax.broadcasted_iota(jnp.int32, (rows, rows), 0) < lax.broadcasted_iota(jnp.int32, (rows, rows), 1)
    earlier = jnp.dot(
        jnp.where(belongs, 1.0, 0.0).astype(jnp.bfloat16),
        jnp.where(before, 1.0, 0.0).astype(jnp.bfloat16),
        preferred_element_type=jnp.float32,
    )
    rank = jnp.sum(jnp.where(belongs, earlier, 0.0), axis=0, keepdims=True).astype(jnp.int32)
    slot = owner * cap + rank
    place = me * cap + rank
    at_place = jnp.where(lax.broadcasted_iota(jnp.int32, (slots, rows), 0) == place, 1.0, 0.0).astype(jnp.bfloat16)

    marks = jnp.where(belongs, (cluster + 1).astype(jnp.float32), 0.0).astype(jnp.bfloat16)
    tag_out[...] = lax.dot_general(marks, at_place, NT, preferred_element_type=jnp.float32)

    chunk = rows // 4
    for c in range(4):
        part = pl.ds(c * chunk, chunk)
        normed[part, :] = unit_rows(x_ref[part, :])

    pl.semaphore_wait(barrier, len(partners))

    ztags = []
    for r in (1, 2, 3):
        copy = remote(tag_out, tag_in.at[r - 1], ztag_s.at[r - 1], ztag_r.at[r - 1], (peer[r], tile))
        copy.start()
        ztags.append(copy)

    def filled(group):
        sel = lax.broadcasted_iota(jnp.int32, (cap, rows), 0) + group * cap
        sel = jnp.where(sel == slot, 1.0, 0.0).astype(jnp.bfloat16)
        return jnp.dot(sel, normed[...], preferred_element_type=jnp.float32).astype(jnp.bfloat16)

    def piece(r):
        return pl.ds(pl.multiple_of(peer[r] * cap, cap), cap)

    def zcopy(r):
        return remote(send.at[r - 1], members.at[0, piece(0), :], z_s.at[r - 1], z_r.at[r - 1], (peer[r], tile))

    def spread(r):
        src = members.at[0, piece(r), :]
        copies = [
            remote(src, members.at[1, piece(r), :], sib_s.at[r], sib_r.at[r], (me, sib)),
            remote(src, members.at[2, piece(r), :], near_s.at[0, r], near_r.at[0, r], (me, xdev)),
            remote(src, members.at[3, piece(r), :], near_s.at[1, r], near_r.at[1, r], (me, ydev)),
        ]
        for copy in copies[::-1]:
            copy.start()
        return copies

    def relay(r, copies):
        copies[2].wait_recv()
        copy = remote(members.at[3, piece(r), :], members.at[4, piece(r), :], relay_s.at[r], relay_r.at[r], (me, sib))
        copy.start()
        return copy

    zcopies = {}
    for r in (2, 1):
        send[r - 1] = filled(peer[r])
        zcopies[r] = zcopy(r)
        zcopies[r].start()
    members[0, piece(0), :] = filled(me)
    spreads, relays = [spread(0)], []
    send[2] = filled(peer[3])

    for copy in ztags:
        copy.wait_recv()
    total = tag_out[...] + tag_in[0] + tag_in[1] + tag_in[2]
    tags[0] = jnp.sum(
        jnp.where(lax.broadcasted_iota(jnp.int32, (8, slots), 0) == me, total, 0.0), axis=0, keepdims=True
    )
    ptags = []
    for n, device in enumerate((sib, xdev, ydev, ydev + beside)):
        copy = remote(tags.at[0], tags.at[1 + n], ptag_s.at[n], ptag_r.at[n], (me, device))
        copy.start()
        ptags.append(copy)

    zcopies[2].wait_send()
    zcopies[3] = zcopy(3)
    zcopies[3].start()
    zcopies[1].wait_recv()
    spreads.append(spread(1))
    zcopies[2].wait_recv()
    spreads.append(spread(2))
    relays.append(relay(0, spreads[0]))

    for copy in ptags:
        copy.wait_recv()
    best[...] = jnp.full(best.shape, -1.0, jnp.float32)
    for n in range(5):
        row = tags[n]
        query_tags[n, 0] = row[:, :half]
        query_tags[n, 1] = row[:, half:]
        for i in range(groups):
            first = i * cap // 128 * 128
            lanes = lax.broadcasted_iota(jnp.int32, (cap, 256), 1) + (first - i * cap)
            wanted = lax.broadcasted_iota(jnp.int32, (cap, 256), 0)
            picked = jnp.sum(jnp.where(lanes == wanted, row[:, first : first + 256], 0.0), axis=1, keepdims=True)
            picked = jnp.where(picked > 0.0, picked, -1.0)
            key_tags[n, i * cap : (i + 1) * cap, :] = jnp.broadcast_to(picked, (cap, 128))

    def compare(kblock, khalf, qblock, qhalf, to, own=False):
        lines = pl.ds(pl.multiple_of(khalf * half, half), half)
        asked = members[qblock, pl.ds(pl.multiple_of(qhalf * half, half), half), :]
        scores = lax.dot_general(members[kblock, lines, :], asked, NT, preferred_element_type=jnp.float32)
        key_tag = jnp.concatenate([key_tags[kblock, lines, :]] * (half // 128), axis=1)
        allowed = key_tag == query_tags[qblock, qhalf]
        if own:
            line = lax.broadcasted_iota(jnp.int32, (half, half), 0) + (khalf * half + (kblock + qblock) * 2 * slots)
            lane = lax.broadcasted_iota(jnp.int32, (half, half), 1) + qhalf * half
            allowed = allowed & (line != lane)
        found = jnp.max(jnp.where(allowed, scores, -1.0), axis=0, keepdims=True)
        best[to, qhalf] = jnp.maximum(best[to, qhalf], found)

    relays.append(relay(1, spreads[1]))
    for copies in spreads[:2]:
        copies[0].wait_recv()
        copies[1].wait_recv()

    @pl.loop(0, 6)
    def _(i):
        j = i // 2
        q = lax.rem(i, 2)
        compare(j + (j + 1) // 2, early, q, early, q, own=True)

    for copy in relays[:2]:
        copy.wait_recv()

    @pl.loop(0, 2)
    def _(q):
        compare(cross + q * (2 - cross), early, 2 + q * (cross - 2), early, 2 + q)

    relays.append(relay(2, spreads[2]))
    zcopies[3].wait_recv()
    spreads.append(spread(3))
    for copies in spreads[2:]:
        copies[0].wait_recv()

    @pl.loop(0, 6)
    def _(i):
        j = i // 2
        q = lax.rem(i, 2)
        compare(j + (j + 1) // 2, early, q, late, q, own=True)

    @pl.loop(0, 4)
    def _(i):
        q = lax.rem(i, 2)
        compare(0, late, q, i // 2, q, own=True)

    relays.append(relay(3, spreads[3]))
    for copies in spreads[2:]:
        copies[1].wait_recv()

    @pl.loop(0, 8)
    def _(i):
        q = lax.rem(i, 2)
        compare(2 + i // 4, late, q, lax.rem(i // 2, 2), q)

    for copy in relays[2:]:
        copy.wait_recv()

    @pl.loop(0, 6)
    def _(i):
        q = lax.rem(i, 2)
        m = i // 2
        compare(
            cross + q * (2 - cross), early + (late - early) * (1 - lax.rem(m, 2)),
            2 + q * (cross - 2), early + (late - early) * ((m + 1) // 2), 2 + q,
        )

    copies = []
    for h, device in enumerate((tile, sib, xdev, crossdev)):
        result_out[h] = jnp.concatenate([best[h, 0], best[h, 1]], axis=1)
        for r in (3, 2, 1, 0):
            index = h * 4 + r
            if index == 0:
                result_in[0] = result_out[0]
                continue
            copy = remote(
                result_out.at[h], result_in.at[index], res_s.at[index], res_r.at[index], (peer[r], device)
            )
            copy.start()
            copies.append(copy)
    for copy in copies:
        copy.wait_recv()

    picks[...] = jnp.zeros(picks.shape, jnp.float32)
    for r in range(4):
        block = jnp.maximum(
            jnp.maximum(result_in[r], result_in[4 + r]), jnp.maximum(result_in[8 + r], result_in[12 + r])
        )
        high = block.astype(jnp.bfloat16).astype(jnp.float32)
        middle = (block - high).astype(jnp.bfloat16).astype(jnp.float32)
        picks[r : r + 1, :] = high
        picks[4 + r : 5 + r, :] = middle
        picks[8 + r : 9 + r, :] = (block - high) - middle
    found = jnp.dot(picks[...].astype(jnp.bfloat16), at_place, preferred_element_type=jnp.float32)
    out = jnp.zeros((1, rows), jnp.float32)
    for r in range(4):
        value = (found[r : r + 1, :] + found[4 + r : 5 + r, :]) + found[8 + r : 9 + r, :]
        out = jnp.where(owner == peer[r], value, out)
    out_ref[...] = out

    for copy in ztags + ptags + copies + relays + [zcopies[1], zcopies[3]]:
        copy.wait_send()
    for group in spreads:
        for copy in group:
            copy.wait_send()


def local_fused(embeddings, row_group, row_cluster):
    rows, columns = embeddings.shape
    slots = 2 * rows
    dma = pltpu.SemaphoreType.DMA
    out = pl.pallas_call(
        kernel,
        out_shape=jax.ShapeDtypeStruct((1, rows), jnp.float32),
        in_specs=[pl.BlockSpec(memory_space=pltpu.VMEM)] * 3,
        out_specs=pl.BlockSpec(memory_space=pltpu.VMEM),
        scratch_shapes=[
            pltpu.VMEM((rows, columns), jnp.bfloat16),
            pltpu.VMEM((3, slots // 4, columns), jnp.bfloat16),
            pltpu.VMEM((5, slots, columns), jnp.bfloat16),
            pltpu.VMEM((8, slots), jnp.float32),
            pltpu.VMEM((3, 8, slots), jnp.float32),
            pltpu.VMEM((5, 1, slots), jnp.float32),
            pltpu.VMEM((5, 2, 1, slots // 2), jnp.float32),
            pltpu.VMEM((5, slots, 128), jnp.float32),
            pltpu.VMEM((4, 2, 1, slots // 2), jnp.float32),
            pltpu.VMEM((4, 1, slots), jnp.float32),
            pltpu.VMEM((16, 1, slots), jnp.float32),
            pltpu.VMEM((16, slots), jnp.float32),
            dma((3,)), dma((3,)), dma((3,)), dma((3,)),
            dma((4,)), dma((4,)), dma((4,)), dma((4,)),
            dma((2, 4)), dma((2, 4)), dma((4,)), dma((4,)),
            dma((16,)), dma((16,)),
        ],
        compiler_params=pltpu.CompilerParams(
            collective_id=0, has_side_effects=True, vmem_limit_bytes=48 * 1024 * 1024
        ),
    )(embeddings, row_group.reshape(1, rows), row_cluster.reshape(1, rows))
    return out.reshape(rows)


def solution(mesh):
    fused = mesh.shape["grp"] == 4 and mesh.shape["tile"] == 8
    placed = (P(("grp", "tile"), None), P(("grp", "tile")), P(("grp", "tile")))
    return jax.shard_map(
        local_fused if fused else local_general,
        mesh=mesh, in_specs=placed, out_specs=P(("grp", "tile")), check_vma=False,
    )
```

```python
import jax
import jax.numpy as jnp
from jax import lax
from jax.experimental import pallas as pl
from jax.experimental.pallas import tpu as pltpu
from jax.sharding import PartitionSpec as P

MESH = pl.DeviceIdType.MESH
epsilon = 1e-06
NT = (((1,), (1,)), ((), ()))


def unit_rows(values):
    floats = values.astype(jnp.float32)
    scaled = floats * lax.rsqrt(jnp.sum(floats * floats, axis=-1, keepdims=True) + epsilon)
    return scaled.astype(jnp.bfloat16)


def slot_index(owners, groups, capacity):
    onehot = (owners[:, None] == jnp.arange(groups, dtype=jnp.int32)[None, :]).astype(jnp.int32)
    earlier = jnp.cumsum(onehot, axis=0) - onehot
    ranked = jnp.sum(earlier * onehot, axis=1)
    return owners * capacity + ranked


def masked_table(scores, left_ids, right_ids, left_pos, right_pos):
    allowed = (
        (left_ids[:, None] == right_ids[None, :])
        & (right_ids[None, :] >= 0)
        & (left_pos[:, None] != right_pos[None, :])
    )
    return jnp.where(allowed, scores, jnp.float32(-1.0))


def local_general(embeddings, row_group, row_cluster):
    row_count = embeddings.shape[0]
    columns = embeddings.shape[1]
    groups = lax.axis_size("grp")
    capacity = 2 * row_count // groups
    slots_all = groups * capacity
    placed = slot_index(row_group, groups, capacity)
    normed = unit_rows(embeddings)
    outgoing = (
        jnp.zeros((slots_all, columns), jnp.bfloat16)
        .at[placed]
        .set(normed)
        .reshape(groups, capacity, columns)
    )
    out_tags = (
        jnp.full((slots_all,), -1, jnp.int32).at[placed].set(row_cluster).reshape(groups, capacity)
    )
    members, member_ids = (
        lax.all_to_all(outgoing, "grp", split_axis=0, concat_axis=0, tiled=True),
        lax.all_to_all(out_tags, "grp", split_axis=0, concat_axis=0, tiled=True),
    )
    members = members.reshape(slots_all, columns)
    member_ids = member_ids.reshape(slots_all)
    tile_here = lax.axis_index("tile")
    local_pos = jnp.arange(slots_all, dtype=jnp.int32)
    own_pos = tile_here * slots_all + local_pos
    start_best = jnp.full((slots_all,), -1.0, jnp.float32)
    piece_rows = lax.all_gather(members, "tile", axis=0, tiled=True)
    piece_ids = lax.all_gather(member_ids, "tile", axis=0, tiled=True)
    scores = jnp.einsum("id,jd->ij", members, piece_rows, preferred_element_type=jnp.float32)
    piece_pos = jnp.arange(piece_rows.shape[0], dtype=jnp.int32)
    best_sim = jnp.maximum(
        start_best, jnp.max(masked_table(scores, member_ids, piece_ids, own_pos, piece_pos), axis=1)
    )
    results = best_sim.reshape(groups, capacity)
    arrived = lax.all_to_all(results, "grp", split_axis=0, concat_axis=0, tiled=True)
    return jnp.take(arrived.reshape(slots_all), placed)


def kernel(
    x_ref, owner_ref, cluster_ref, out_ref,
    loaded, normed, send, members, tag_out, tag_in, tags, key_tags, best, result_in, picks, load_s,
    ztag_s, ztag_r, z_s, z_r, ptag_s, ptag_r, sib_s, sib_r, near_s, near_r, relay_s, relay_r, res_s, res_r,
):
    rows = x_ref.shape[0]
    groups = 4
    cap = 2 * rows // groups
    slots = groups * cap
    half = cap // 2
    early = 3 * cap
    me = lax.axis_index("grp")
    tile = lax.axis_index("tile")
    core = lax.rem(tile, 2)
    xpos = lax.rem(tile // 2, 2)
    ypos = tile // 4
    beside = 1 - 2 * core
    sib = tile + beside
    xdev = tile + 2 - 4 * xpos
    ydev = tile + 4 - 8 * ypos
    cross = 4 - xpos
    crossdev = ydev + (1 - xpos) * beside
    peer = (me, me + 1 - 2 * lax.rem(me, 2), me + 2 - 4 * (me // 2), 3 - me)

    partners = [(peer[r], tile) for r in (1, 2, 3)]
    partners += [(peer[r], device) for r in range(4) for device in (sib, xdev, ydev, ydev + beside)]
    barrier = pltpu.get_barrier_semaphore()
    for partner in partners:
        pl.semaphore_signal(barrier, inc=1, device_id=partner, device_id_type=MESH)

    load = pltpu.make_async_copy(x_ref, loaded, load_s)
    load.start()

    def remote(src, dst, ssem, rsem, device):
        return pltpu.make_async_remote_copy(
            src_ref=src, dst_ref=dst, send_sem=ssem, recv_sem=rsem, device_id=device, device_id_type=MESH
        )

    owner = owner_ref[...].reshape(1, rows)
    cluster = cluster_ref[...].reshape(1, rows)
    group_of = lax.broadcasted_iota(jnp.int32, (8, rows), 0)
    belongs = group_of == owner
    before = lax.broadcasted_iota(jnp.int32, (rows, rows), 0) < lax.broadcasted_iota(jnp.int32, (rows, rows), 1)
    earlier = jnp.dot(
        jnp.where(belongs, 1.0, 0.0).astype(jnp.bfloat16),
        jnp.where(before, 1.0, 0.0).astype(jnp.bfloat16),
        preferred_element_type=jnp.float32,
    )
    rank = jnp.sum(jnp.where(belongs, earlier, 0.0), axis=0, keepdims=True).astype(jnp.int32)
    slot = owner * cap + rank
    at_rank = jnp.where(lax.broadcasted_iota(jnp.int32, (cap, rows), 0) == rank, 1.0, 0.0).astype(jnp.bfloat16)

    load.wait()
    chunk = rows // 4
    for c in range(4):
        part = pl.ds(c * chunk, chunk)
        normed[part, :] = unit_rows(loaded[part, :])

    def filled(group):
        sel = lax.broadcasted_iota(jnp.int32, (cap, rows), 0) + group * cap
        sel = jnp.where(sel == slot, 1.0, 0.0).astype(jnp.bfloat16)
        return jnp.dot(sel, normed[...], preferred_element_type=jnp.float32).astype(jnp.bfloat16)

    def zcopy(r, p):
        part = 2 * r + p
        return remote(
            send.at[r - 1, pl.ds(p * half, half), :], members.at[0, pl.ds(part * half, half), :],
            z_s.at[part], z_r.at[part], (peer[r], tile),
        )

    def spread(r, p):
        part = 2 * r + p
        line = pl.ds(part * half, half)
        src = members.at[0, line, :]
        copies = [
            remote(src, members.at[1, line, :], sib_s.at[part], sib_r.at[part], (me, sib)),
            remote(src, members.at[2, line, :], near_s.at[0, part], near_r.at[0, part], (me, xdev)),
            remote(src, members.at[3, line, :], near_s.at[1, part], near_r.at[1, part], (me, ydev)),
        ]
        for copy in copies[::-1]:
            copy.start()
        return copies

    def relay(part, copies):
        copies[2].wait_recv()
        line = pl.ds(part * half, half)
        copy = remote(members.at[3, line, :], members.at[4, line, :], relay_s.at[part], relay_r.at[part], (me, sib))
        copy.start()
        return copy

    zcopies = {}

    def begin(r, p):
        zcopies[r, p] = zcopy(r, p)
        zcopies[r, p].start()

    send[1] = filled(peer[2])
    pl.semaphore_wait(barrier, len(partners))
    begin(2, 0)
    send[0] = filled(peer[1])
    begin(1, 0)
    members[0, 0:cap, :] = filled(me)
    spreads, relays = [spread(0, 0), spread(0, 1)], []
    send[2] = filled(peer[3])

    marks = jnp.where(belongs, (cluster + 1).astype(jnp.float32), 0.0).astype(jnp.bfloat16)
    marked = lax.dot_general(marks, at_rank, NT, preferred_element_type=jnp.float32)
    tag_out[...] = jnp.zeros(tag_out.shape, jnp.float32)
    ztags = []
    for r in range(4):
        tag_out[r, :, r * cap : (r + 1) * cap] = marked
        if r:
            copy = remote(tag_out.at[r], tag_in.at[r - 1], ztag_s.at[r - 1], ztag_r.at[r - 1], (peer[r], tile))
            copy.start()
            ztags.append(copy)

    zcopies[2, 0].wait_send()
    begin(2, 1)
    zcopies[1, 0].wait_send()
    begin(1, 1)

    for copy in ztags:
        copy.wait_recv()
    total = tag_out[0] + tag_in[0] + tag_in[1] + tag_in[2]
    tags[0] = jnp.sum(
        jnp.where(lax.broadcasted_iota(jnp.int32, (8, slots), 0) == me, total, 0.0), axis=0, keepdims=True
    )
    ptags = []
    for n, device in enumerate((sib, xdev, ydev, ydev + beside)):
        copy = remote(tags.at[0], tags.at[1 + n], ptag_s.at[n], ptag_r.at[n], (me, device))
        copy.start()
        ptags.append(copy)

    zcopies[1, 0].wait_recv()
    spreads.append(spread(1, 0))
    zcopies[2, 0].wait_recv()
    spreads.append(spread(2, 0))
    zcopies[2, 1].wait_send()
    begin(3, 0)
    zcopies[1, 1].wait_recv()
    spreads.append(spread(1, 1))
    zcopies[2, 1].wait_recv()
    spreads.append(spread(2, 1))
    parts = [0, 1, 2, 4, 3, 5, 6, 7]

    for copy in ptags:
        copy.wait_recv()
    best[...] = jnp.full(best.shape, -1.0, jnp.float32)
    for n in range(5):
        for i in range(groups):
            first = i * cap // 128 * 128
            lanes = lax.broadcasted_iota(jnp.int32, (cap, 256), 1) + (first - i * cap)
            wanted = lax.broadcasted_iota(jnp.int32, (cap, 256), 0)
            picked = jnp.sum(
                jnp.where(lanes == wanted, tags[n, :, first : first + 256], 0.0), axis=1, keepdims=True
            )
            picked = jnp.where(picked > 0.0, picked, -1.0)
            key_tags[n, i * cap : (i + 1) * cap, :] = jnp.broadcast_to(picked, (cap, 128))

    def compare(kblock, keys, qblock, queries, to, own=False):
        (k0, k1), (q0, q1) = keys, queries
        shape = (k1 - k0, q1 - q0)
        scores = lax.dot_general(
            members[kblock, k0:k1, :], members[qblock, q0:q1, :], NT, preferred_element_type=jnp.float32
        )
        allowed = key_tags[kblock, k0:k1, 0:1] == tags[qblock, :, q0:q1]
        if own:
            line = lax.broadcasted_iota(jnp.int32, shape, 0) + (k0 + (kblock + qblock) * 2 * slots)
            lane = lax.broadcasted_iota(jnp.int32, shape, 1) + q0
            allowed = allowed & (line != lane)
        found = jnp.max(jnp.where(allowed, scores, -1.0), axis=0, keepdims=True)
        best[to, :, q0:q1] = jnp.maximum(best[to, :, q0:q1], found)

    first, last, whole = (0, early), (early, slots), (0, slots)

    for n in (0, 1, 2):
        relays.append(relay(parts[n], spreads[n]))
    zcopies[3, 0].wait_send()
    begin(3, 1)
    for n in (3, 4, 5):
        relays.append(relay(parts[n], spreads[n]))
    zcopies[3, 0].wait_recv()
    spreads.append(spread(3, 0))
    for copies in spreads[:6]:
        copies[0].wait_recv()
        copies[1].wait_recv()

    @pl.loop(0, 6)
    def _(i):
        j = i // 2
        q = lax.rem(i, 2)
        compare(j + (j + 1) // 2, first, q, first, q, own=True)

    zcopies[3, 1].wait_recv()
    spreads.append(spread(3, 1))
    for copy in relays[:6]:
        copy.wait_recv()

    @pl.loop(0, 2)
    def _(q):
        compare(cross + q * (2 - cross), first, 2 + q * (cross - 2), first, 2 + q)

    relays.append(relay(parts[6], spreads[6]))
    for copies in spreads[6:]:
        copies[0].wait_recv()

    @pl.loop(0, 6)
    def _(i):
        j = i // 2
        q = lax.rem(i, 2)
        compare(j + (j + 1) // 2, first, q, last, q, own=True)

    @pl.loop(0, 2)
    def _(q):
        compare(0, last, q, whole, q, own=True)

    relays.append(relay(parts[7], spreads[7]))
    for copies in spreads[6:]:
        copies[1].wait_recv()

    @pl.loop(0, 4)
    def _(i):
        q = lax.rem(i, 2)
        compare(2 + i // 2, last, q, whole, q)

    for copy in relays[6:]:
        copy.wait_recv()

    @pl.loop(0, 2)
    def _(q):
        compare(cross + q * (2 - cross), first, 2 + q * (cross - 2), last, 2 + q)

    @pl.loop(0, 2)
    def _(q):
        compare(cross + q * (2 - cross), last, 2 + q * (cross - 2), whole, 2 + q)

    copies = []
    for h, device in enumerate((tile, sib, xdev, crossdev)):
        for r in (3, 2, 1, 0):
            index = h * 4 + r
            if index == 0:
                result_in[0] = best[0]
                continue
            copy = remote(
                best.at[h], result_in.at[index], res_s.at[index], res_r.at[index], (peer[r], device)
            )
            copy.start()
            copies.append(copy)
    for copy in copies:
        copy.wait_recv()

    picks[...] = jnp.zeros(picks.shape, jnp.float32)
    for r in range(4):
        block = jnp.maximum(
            jnp.maximum(result_in[r], result_in[4 + r]), jnp.maximum(result_in[8 + r], result_in[12 + r])
        )[:, r * cap : (r + 1) * cap]
        high = block.astype(jnp.bfloat16).astype(jnp.float32)
        middle = (block - high).astype(jnp.bfloat16).astype(jnp.float32)
        picks[r : r + 1, :] = high
        picks[4 + r : 5 + r, :] = middle
        picks[8 + r : 9 + r, :] = (block - high) - middle
    found = jnp.dot(picks[...].astype(jnp.bfloat16), at_rank, preferred_element_type=jnp.float32)
    out = jnp.zeros((1, rows), jnp.float32)
    for r in range(4):
        value = (found[r : r + 1, :] + found[4 + r : 5 + r, :]) + found[8 + r : 9 + r, :]
        out = jnp.where(owner == peer[r], value, out)
    out_ref[...] = out.reshape(rows)

    for copy in ztags + ptags + copies + relays + [zcopies[1, 1], zcopies[3, 1]]:
        copy.wait_send()
    for group in spreads:
        for copy in group:
            copy.wait_send()


def local_fused(embeddings, row_group, row_cluster):
    rows, columns = embeddings.shape
    slots = 2 * rows
    dma = pltpu.SemaphoreType.DMA
    return pl.pallas_call(
        kernel,
        out_shape=jax.ShapeDtypeStruct((rows,), jnp.float32),
        in_specs=[pl.BlockSpec(memory_space=pl.ANY)] + [pl.BlockSpec(memory_space=pltpu.VMEM)] * 2,
        out_specs=pl.BlockSpec(memory_space=pltpu.VMEM),
        scratch_shapes=[
            pltpu.VMEM((rows, columns), jnp.bfloat16),
            pltpu.VMEM((rows, columns), jnp.bfloat16),
            pltpu.VMEM((3, slots // 4, columns), jnp.bfloat16),
            pltpu.VMEM((5, slots, columns), jnp.bfloat16),
            pltpu.VMEM((4, 8, slots), jnp.float32),
            pltpu.VMEM((3, 8, slots), jnp.float32),
            pltpu.VMEM((5, 1, slots), jnp.float32),
            pltpu.VMEM((5, slots, 128), jnp.float32),
            pltpu.VMEM((4, 1, slots), jnp.float32),
            pltpu.VMEM((16, 1, slots), jnp.float32),
            pltpu.VMEM((16, slots // 4), jnp.float32),
            dma(()),
            dma((3,)), dma((3,)), dma((8,)), dma((8,)),
            dma((4,)), dma((4,)), dma((8,)), dma((8,)),
            dma((2, 8)), dma((2, 8)), dma((8,)), dma((8,)),
            dma((16,)), dma((16,)),
        ],
        compiler_params=pltpu.CompilerParams(
            collective_id=0, has_side_effects=True, vmem_limit_bytes=48 * 1024 * 1024
        ),
    )(embeddings, row_group, row_cluster)


def solution(mesh):
    fused = mesh.shape["grp"] == 4 and mesh.shape["tile"] == 8
    placed = (P(("grp", "tile"), None), P(("grp", "tile")), P(("grp", "tile")))
    return jax.shard_map(
        local_fused if fused else local_general,
        mesh=mesh, in_specs=placed, out_specs=P(("grp", "tile")), check_vma=False,
    )
```

```python
import jax
import jax.numpy as jnp
from jax import lax
from jax.experimental import pallas as pl
from jax.experimental.pallas import tpu as pltpu
from jax.sharding import PartitionSpec as P

MESH = pl.DeviceIdType.MESH
epsilon = 1e-06
NT = (((1,), (1,)), ((), ()))


def unit_rows(values):
    floats = values.astype(jnp.float32)
    scaled = floats * lax.rsqrt(jnp.sum(floats * floats, axis=-1, keepdims=True) + epsilon)
    return scaled.astype(jnp.bfloat16)


def slot_index(owners, groups, capacity):
    onehot = (owners[:, None] == jnp.arange(groups, dtype=jnp.int32)[None, :]).astype(jnp.int32)
    earlier = jnp.cumsum(onehot, axis=0) - onehot
    ranked = jnp.sum(earlier * onehot, axis=1)
    return owners * capacity + ranked


def masked_table(scores, left_ids, right_ids, left_pos, right_pos):
    allowed = (
        (left_ids[:, None] == right_ids[None, :])
        & (right_ids[None, :] >= 0)
        & (left_pos[:, None] != right_pos[None, :])
    )
    return jnp.where(allowed, scores, jnp.float32(-1.0))


def local_general(embeddings, row_group, row_cluster):
    row_count = embeddings.shape[0]
    columns = embeddings.shape[1]
    groups = lax.axis_size("grp")
    capacity = 2 * row_count // groups
    slots_all = groups * capacity
    placed = slot_index(row_group, groups, capacity)
    normed = unit_rows(embeddings)
    outgoing = (
        jnp.zeros((slots_all, columns), jnp.bfloat16)
        .at[placed]
        .set(normed)
        .reshape(groups, capacity, columns)
    )
    out_tags = (
        jnp.full((slots_all,), -1, jnp.int32).at[placed].set(row_cluster).reshape(groups, capacity)
    )
    members, member_ids = (
        lax.all_to_all(outgoing, "grp", split_axis=0, concat_axis=0, tiled=True),
        lax.all_to_all(out_tags, "grp", split_axis=0, concat_axis=0, tiled=True),
    )
    members = members.reshape(slots_all, columns)
    member_ids = member_ids.reshape(slots_all)
    tile_here = lax.axis_index("tile")
    local_pos = jnp.arange(slots_all, dtype=jnp.int32)
    own_pos = tile_here * slots_all + local_pos
    start_best = jnp.full((slots_all,), -1.0, jnp.float32)
    piece_rows = lax.all_gather(members, "tile", axis=0, tiled=True)
    piece_ids = lax.all_gather(member_ids, "tile", axis=0, tiled=True)
    scores = jnp.einsum("id,jd->ij", members, piece_rows, preferred_element_type=jnp.float32)
    piece_pos = jnp.arange(piece_rows.shape[0], dtype=jnp.int32)
    best_sim = jnp.maximum(
        start_best, jnp.max(masked_table(scores, member_ids, piece_ids, own_pos, piece_pos), axis=1)
    )
    results = best_sim.reshape(groups, capacity)
    arrived = lax.all_to_all(results, "grp", split_axis=0, concat_axis=0, tiled=True)
    return jnp.take(arrived.reshape(slots_all), placed)


def kernel(
    x_ref, owner_ref, cluster_ref, out_ref,
    loaded, owners, clusters, normed, send, members, tag_out, tag_in, tags, key_tags, best, result_in, picks, load_s,
    ztag_s, ztag_r, z_s, z_r, ptag_s, ptag_r, sib_s, sib_r, near_s, near_r, relay_s, relay_r, res_s, res_r,
):
    rows = x_ref.shape[0]
    groups = 4
    cap = 2 * rows // groups
    slots = groups * cap
    half = cap // 2
    early = 3 * cap
    me = lax.axis_index("grp")
    tile = lax.axis_index("tile")
    core = lax.rem(tile, 2)
    xpos = lax.rem(tile // 2, 2)
    ypos = tile // 4
    beside = 1 - 2 * core
    sib = tile + beside
    xdev = tile + 2 - 4 * xpos
    ydev = tile + 4 - 8 * ypos
    cross = 4 - xpos
    crossdev = ydev + (1 - xpos) * beside
    peer = (me, me + 1 - 2 * lax.rem(me, 2), me + 2 - 4 * (me // 2), 3 - me)

    partners = [(peer[r], tile) for r in (1, 2, 3)]
    partners += [(peer[r], device) for r in range(4) for device in (sib, xdev, ydev, ydev + beside)]
    barrier = pltpu.get_barrier_semaphore()
    for partner in partners:
        pl.semaphore_signal(barrier, inc=1, device_id=partner, device_id_type=MESH)

    loads = [
        pltpu.make_async_copy(src, dst, load_s.at[n])
        for n, (src, dst) in enumerate(((owner_ref, owners), (cluster_ref, clusters), (x_ref, loaded)))
    ]
    for load in loads:
        load.start()

    def remote(src, dst, ssem, rsem, device):
        return pltpu.make_async_remote_copy(
            src_ref=src, dst_ref=dst, send_sem=ssem, recv_sem=rsem, device_id=device, device_id_type=MESH
        )

    loads[0].wait()
    loads[1].wait()
    owner = owners[...].reshape(1, rows)
    cluster = clusters[...].reshape(1, rows)
    group_of = lax.broadcasted_iota(jnp.int32, (8, rows), 0)
    belongs = group_of == owner
    before = lax.broadcasted_iota(jnp.int32, (rows, rows), 0) < lax.broadcasted_iota(jnp.int32, (rows, rows), 1)
    earlier = jnp.dot(
        jnp.where(belongs, 1.0, 0.0).astype(jnp.bfloat16),
        jnp.where(before, 1.0, 0.0).astype(jnp.bfloat16),
        preferred_element_type=jnp.float32,
    )
    rank = jnp.sum(jnp.where(belongs, earlier, 0.0), axis=0, keepdims=True).astype(jnp.int32)
    slot = owner * cap + rank
    at_rank = jnp.where(lax.broadcasted_iota(jnp.int32, (cap, rows), 0) == rank, 1.0, 0.0).astype(jnp.bfloat16)

    loads[2].wait()
    chunk = rows // 4
    for c in range(4):
        part = pl.ds(c * chunk, chunk)
        normed[part, :] = unit_rows(loaded[part, :])

    def filled(group):
        sel = lax.broadcasted_iota(jnp.int32, (cap, rows), 0) + group * cap
        sel = jnp.where(sel == slot, 1.0, 0.0).astype(jnp.bfloat16)
        return jnp.dot(sel, normed[...], preferred_element_type=jnp.float32).astype(jnp.bfloat16)

    def zcopy(r, p):
        part = 2 * r + p
        return remote(
            send.at[r - 1, pl.ds(p * half, half), :], members.at[0, pl.ds(part * half, half), :],
            z_s.at[part], z_r.at[part], (peer[r], tile),
        )

    def spread(r, p):
        part = 2 * r + p
        line = pl.ds(part * half, half)
        src = members.at[0, line, :]
        copies = [
            remote(src, members.at[1, line, :], sib_s.at[part], sib_r.at[part], (me, sib)),
            remote(src, members.at[2, line, :], near_s.at[0, part], near_r.at[0, part], (me, xdev)),
            remote(src, members.at[3, line, :], near_s.at[1, part], near_r.at[1, part], (me, ydev)),
        ]
        for copy in copies[::-1]:
            copy.start()
        return copies

    def relay(part, copies):
        copies[2].wait_recv()
        line = pl.ds(part * half, half)
        copy = remote(members.at[3, line, :], members.at[4, line, :], relay_s.at[part], relay_r.at[part], (me, sib))
        copy.start()
        return copy

    zcopies = {}

    def begin(r, p):
        zcopies[r, p] = zcopy(r, p)
        zcopies[r, p].start()

    send[1] = filled(peer[2])
    pl.semaphore_wait(barrier, len(partners))
    begin(2, 0)
    begin(2, 1)
    send[0] = filled(peer[1])
    begin(1, 0)
    begin(1, 1)
    members[0, 0:cap, :] = filled(me)
    spreads, relays = [spread(0, 0), spread(0, 1)], []
    send[2] = filled(peer[3])

    marks = jnp.where(belongs, (cluster + 1).astype(jnp.float32), 0.0).astype(jnp.bfloat16)
    marked = lax.dot_general(marks, at_rank, NT, preferred_element_type=jnp.float32)
    tag_out[...] = jnp.zeros(tag_out.shape, jnp.float32)
    ztags = []
    for r in range(4):
        tag_out[r, :, r * cap : (r + 1) * cap] = marked
        if r:
            copy = remote(tag_out.at[r], tag_in.at[r - 1], ztag_s.at[r - 1], ztag_r.at[r - 1], (peer[r], tile))
            copy.start()
            ztags.append(copy)

    for copy in ztags:
        copy.wait_recv()
    total = tag_out[0] + tag_in[0] + tag_in[1] + tag_in[2]
    tags[0] = jnp.sum(
        jnp.where(lax.broadcasted_iota(jnp.int32, (8, slots), 0) == me, total, 0.0), axis=0, keepdims=True
    )
    ptags = []
    for n, device in enumerate((sib, xdev, ydev, ydev + beside)):
        copy = remote(tags.at[0], tags.at[1 + n], ptag_s.at[n], ptag_r.at[n], (me, device))
        copy.start()
        ptags.append(copy)

    zcopies[1, 0].wait_recv()
    spreads.append(spread(1, 0))
    zcopies[2, 0].wait_send()
    begin(3, 0)
    zcopies[2, 0].wait_recv()
    spreads.append(spread(2, 0))
    zcopies[1, 1].wait_recv()
    spreads.append(spread(1, 1))
    zcopies[2, 1].wait_send()
    begin(3, 1)
    zcopies[2, 1].wait_recv()
    spreads.append(spread(2, 1))
    parts = [0, 1, 2, 4, 3, 5, 6, 7]

    for copy in ptags:
        copy.wait_recv()
    best[...] = jnp.full(best.shape, -1.0, jnp.float32)
    for n in range(5):
        for i in range(groups):
            first = i * cap // 128 * 128
            lanes = lax.broadcasted_iota(jnp.int32, (cap, 256), 1) + (first - i * cap)
            wanted = lax.broadcasted_iota(jnp.int32, (cap, 256), 0)
            picked = jnp.sum(
                jnp.where(lanes == wanted, tags[n, :, first : first + 256], 0.0), axis=1, keepdims=True
            )
            picked = jnp.where(picked > 0.0, picked, -1.0)
            key_tags[n, i * cap : (i + 1) * cap, :] = jnp.broadcast_to(picked, (cap, 128))

    def compare(kblock, keys, qblock, queries, to, own=False):
        (k0, k1), (q0, q1) = keys, queries
        shape = (k1 - k0, q1 - q0)
        scores = lax.dot_general(
            members[kblock, k0:k1, :], members[qblock, q0:q1, :], NT, preferred_element_type=jnp.float32
        )
        allowed = key_tags[kblock, k0:k1, 0:1] == tags[qblock, :, q0:q1]
        if own:
            line = lax.broadcasted_iota(jnp.int32, shape, 0) + (k0 + (kblock + qblock) * 2 * slots)
            lane = lax.broadcasted_iota(jnp.int32, shape, 1) + q0
            allowed = allowed & (line != lane)
        found = jnp.max(jnp.where(allowed, scores, -1.0), axis=0, keepdims=True)
        best[to, :, q0:q1] = jnp.maximum(best[to, :, q0:q1], found)

    first, last, whole = (0, early), (early, slots), (0, slots)

    for copies in spreads[:6]:
        copies[0].wait_recv()

    @pl.loop(0, 2)
    def _(q):
        compare(0, first, q, first, q, own=True)

    for n in (0, 1, 2, 3):
        relays.append(relay(parts[n], spreads[n]))
    zcopies[3, 0].wait_recv()
    spreads.append(spread(3, 0))
    for n in (4, 5):
        relays.append(relay(parts[n], spreads[n]))
    for copies in spreads[:6]:
        copies[1].wait_recv()

    @pl.loop(0, 4)
    def _(i):
        q = lax.rem(i, 2)
        compare(2 + i // 2, first, q, first, q)

    zcopies[3, 1].wait_recv()
    spreads.append(spread(3, 1))
    for copy in relays[:6]:
        copy.wait_recv()

    @pl.loop(0, 2)
    def _(q):
        compare(cross + q * (2 - cross), first, 2 + q * (cross - 2), first, 2 + q)

    relays.append(relay(parts[6], spreads[6]))
    for copies in spreads[6:]:
        copies[0].wait_recv()

    @pl.loop(0, 6)
    def _(i):
        j = i // 2
        q = lax.rem(i, 2)
        compare(j + (j + 1) // 2, first, q, last, q, own=True)

    @pl.loop(0, 2)
    def _(q):
        compare(0, last, q, whole, q, own=True)

    relays.append(relay(parts[7], spreads[7]))
    for copies in spreads[6:]:
        copies[1].wait_recv()

    @pl.loop(0, 4)
    def _(i):
        q = lax.rem(i, 2)
        compare(2 + i // 2, last, q, whole, q)

    for copy in relays[6:]:
        copy.wait_recv()

    @pl.loop(0, 2)
    def _(q):
        compare(cross + q * (2 - cross), first, 2 + q * (cross - 2), last, 2 + q)

    @pl.loop(0, 2)
    def _(q):
        compare(cross + q * (2 - cross), last, 2 + q * (cross - 2), whole, 2 + q)

    copies = []
    for h, device in enumerate((tile, sib, xdev, crossdev)):
        for r in (3, 2, 1, 0):
            index = h * 4 + r
            if index == 0:
                result_in[0] = best[0]
                continue
            copy = remote(
                best.at[h], result_in.at[index], res_s.at[index], res_r.at[index], (peer[r], device)
            )
            copy.start()
            copies.append(copy)
    for copy in copies:
        copy.wait_recv()

    picks[...] = jnp.zeros(picks.shape, jnp.float32)
    for r in range(4):
        block = jnp.maximum(
            jnp.maximum(result_in[r], result_in[4 + r]), jnp.maximum(result_in[8 + r], result_in[12 + r])
        )[:, r * cap : (r + 1) * cap]
        high = block.astype(jnp.bfloat16).astype(jnp.float32)
        middle = (block - high).astype(jnp.bfloat16).astype(jnp.float32)
        picks[r : r + 1, :] = high
        picks[4 + r : 5 + r, :] = middle
        picks[8 + r : 9 + r, :] = (block - high) - middle
    found = jnp.dot(picks[...].astype(jnp.bfloat16), at_rank, preferred_element_type=jnp.float32)
    out = jnp.zeros((1, rows), jnp.float32)
    for r in range(4):
        value = (found[r : r + 1, :] + found[4 + r : 5 + r, :]) + found[8 + r : 9 + r, :]
        out = jnp.where(owner == peer[r], value, out)
    out_ref[...] = out.reshape(rows)

    for copy in ztags + ptags + copies + relays + [zcopies[1, 0], zcopies[1, 1], zcopies[3, 0], zcopies[3, 1]]:
        copy.wait_send()
    for group in spreads:
        for copy in group:
            copy.wait_send()


def local_fused(embeddings, row_group, row_cluster):
    rows, columns = embeddings.shape
    slots = 2 * rows
    dma = pltpu.SemaphoreType.DMA
    return pl.pallas_call(
        kernel,
        out_shape=jax.ShapeDtypeStruct((rows,), jnp.float32),
        in_specs=[pl.BlockSpec(memory_space=pltpu.HBM)] * 3,
        out_specs=pl.BlockSpec(memory_space=pltpu.VMEM),
        scratch_shapes=[
            pltpu.VMEM((rows, columns), jnp.bfloat16),
            pltpu.VMEM((rows,), jnp.int32),
            pltpu.VMEM((rows,), jnp.int32),
            pltpu.VMEM((rows, columns), jnp.bfloat16),
            pltpu.VMEM((3, slots // 4, columns), jnp.bfloat16),
            pltpu.VMEM((5, slots, columns), jnp.bfloat16),
            pltpu.VMEM((4, 8, slots), jnp.float32),
            pltpu.VMEM((3, 8, slots), jnp.float32),
            pltpu.VMEM((5, 1, slots), jnp.float32),
            pltpu.VMEM((5, slots, 128), jnp.float32),
            pltpu.VMEM((4, 1, slots), jnp.float32),
            pltpu.VMEM((16, 1, slots), jnp.float32),
            pltpu.VMEM((16, slots // 4), jnp.float32),
            dma((3,)),
            dma((3,)), dma((3,)), dma((8,)), dma((8,)),
            dma((4,)), dma((4,)), dma((8,)), dma((8,)),
            dma((2, 8)), dma((2, 8)), dma((8,)), dma((8,)),
            dma((16,)), dma((16,)),
        ],
        compiler_params=pltpu.CompilerParams(
            collective_id=0, has_side_effects=True, vmem_limit_bytes=48 * 1024 * 1024
        ),
    )(embeddings, row_group, row_cluster)


def solution(mesh):
    fused = mesh.shape["grp"] == 4 and mesh.shape["tile"] == 8
    placed = (P(("grp", "tile"), None), P(("grp", "tile")), P(("grp", "tile")))
    return jax.shard_map(
        local_fused if fused else local_general,
        mesh=mesh, in_specs=placed, out_specs=P(("grp", "tile")), check_vma=False,
    )
```

```python
import jax
import jax.numpy as jnp
from jax import lax
from jax.experimental import pallas as pl
from jax.experimental.pallas import tpu as pltpu
from jax.sharding import PartitionSpec as P

MESH = pl.DeviceIdType.MESH
epsilon = 1e-06
NT = (((1,), (1,)), ((), ()))


def unit_rows(values):
    floats = values.astype(jnp.float32)
    scaled = floats * lax.rsqrt(jnp.sum(floats * floats, axis=-1, keepdims=True) + epsilon)
    return scaled.astype(jnp.bfloat16)


def slot_index(owners, groups, capacity):
    onehot = (owners[:, None] == jnp.arange(groups, dtype=jnp.int32)[None, :]).astype(jnp.int32)
    earlier = jnp.cumsum(onehot, axis=0) - onehot
    ranked = jnp.sum(earlier * onehot, axis=1)
    return owners * capacity + ranked


def masked_table(scores, left_ids, right_ids, left_pos, right_pos):
    allowed = (
        (left_ids[:, None] == right_ids[None, :])
        & (right_ids[None, :] >= 0)
        & (left_pos[:, None] != right_pos[None, :])
    )
    return jnp.where(allowed, scores, jnp.float32(-1.0))


def local_general(embeddings, row_group, row_cluster):
    row_count = embeddings.shape[0]
    columns = embeddings.shape[1]
    groups = lax.axis_size("grp")
    capacity = 2 * row_count // groups
    slots_all = groups * capacity
    placed = slot_index(row_group, groups, capacity)
    normed = unit_rows(embeddings)
    outgoing = (
        jnp.zeros((slots_all, columns), jnp.bfloat16)
        .at[placed]
        .set(normed)
        .reshape(groups, capacity, columns)
    )
    out_tags = (
        jnp.full((slots_all,), -1, jnp.int32).at[placed].set(row_cluster).reshape(groups, capacity)
    )
    members, member_ids = (
        lax.all_to_all(outgoing, "grp", split_axis=0, concat_axis=0, tiled=True),
        lax.all_to_all(out_tags, "grp", split_axis=0, concat_axis=0, tiled=True),
    )
    members = members.reshape(slots_all, columns)
    member_ids = member_ids.reshape(slots_all)
    tile_here = lax.axis_index("tile")
    local_pos = jnp.arange(slots_all, dtype=jnp.int32)
    own_pos = tile_here * slots_all + local_pos
    start_best = jnp.full((slots_all,), -1.0, jnp.float32)
    piece_rows = lax.all_gather(members, "tile", axis=0, tiled=True)
    piece_ids = lax.all_gather(member_ids, "tile", axis=0, tiled=True)
    scores = jnp.einsum("id,jd->ij", members, piece_rows, preferred_element_type=jnp.float32)
    piece_pos = jnp.arange(piece_rows.shape[0], dtype=jnp.int32)
    best_sim = jnp.maximum(
        start_best, jnp.max(masked_table(scores, member_ids, piece_ids, own_pos, piece_pos), axis=1)
    )
    results = best_sim.reshape(groups, capacity)
    arrived = lax.all_to_all(results, "grp", split_axis=0, concat_axis=0, tiled=True)
    return jnp.take(arrived.reshape(slots_all), placed)


def kernel(
    x_ref, owner_ref, cluster_ref, out_ref,
    loaded, owners, clusters, normed, send, members, tag_out, tag_in, tags, key_tags, best, result_in, picks, load_s,
    ztag_s, ztag_r, z_s, z_r, ptag_s, ptag_r, sib_s, sib_r, near_s, near_r, relay_s, relay_r, res_s, res_r,
):
    rows = x_ref.shape[0]
    groups = 4
    cap = 2 * rows // groups
    slots = groups * cap
    half = cap // 2
    early = 3 * cap
    me = lax.axis_index("grp")
    tile = lax.axis_index("tile")
    core = lax.rem(tile, 2)
    xpos = lax.rem(tile // 2, 2)
    ypos = tile // 4
    beside = 1 - 2 * core
    sib = tile + beside
    xdev = tile + 2 - 4 * xpos
    ydev = tile + 4 - 8 * ypos
    cross = 4 - xpos
    crossdev = ydev + (1 - xpos) * beside
    peer = (me, me + 1 - 2 * lax.rem(me, 2), me + 2 - 4 * (me // 2), 3 - me)

    partners = [(peer[r], tile) for r in (1, 2, 3)]
    partners += [(peer[r], device) for r in range(4) for device in (sib, xdev, ydev, ydev + beside)]
    barrier = pltpu.get_barrier_semaphore()
    for partner in partners:
        pl.semaphore_signal(barrier, inc=1, device_id=partner, device_id_type=MESH)

    loads = [
        pltpu.make_async_copy(src, dst, load_s.at[n])
        for n, (src, dst) in enumerate(((owner_ref, owners), (cluster_ref, clusters), (x_ref, loaded)))
    ]
    for load in loads:
        load.start()

    def remote(src, dst, ssem, rsem, device):
        return pltpu.make_async_remote_copy(
            src_ref=src, dst_ref=dst, send_sem=ssem, recv_sem=rsem, device_id=device, device_id_type=MESH
        )

    loads[0].wait()
    loads[1].wait()
    owner = owners[...].reshape(1, rows)
    cluster = clusters[...].reshape(1, rows)
    group_of = lax.broadcasted_iota(jnp.int32, (8, rows), 0)
    belongs = group_of == owner
    before = lax.broadcasted_iota(jnp.int32, (rows, rows), 0) < lax.broadcasted_iota(jnp.int32, (rows, rows), 1)
    earlier = jnp.dot(
        jnp.where(belongs, 1.0, 0.0).astype(jnp.bfloat16),
        jnp.where(before, 1.0, 0.0).astype(jnp.bfloat16),
        preferred_element_type=jnp.float32,
    )
    rank = jnp.sum(jnp.where(belongs, earlier, 0.0), axis=0, keepdims=True).astype(jnp.int32)
    slot = owner * cap + rank
    at_rank = jnp.where(lax.broadcasted_iota(jnp.int32, (cap, rows), 0) == rank, 1.0, 0.0).astype(jnp.bfloat16)

    loads[2].wait()
    chunk = rows // 4
    for c in range(4):
        part = pl.ds(c * chunk, chunk)
        normed[part, :] = unit_rows(loaded[part, :])

    def filled(group):
        sel = lax.broadcasted_iota(jnp.int32, (cap, rows), 0) + group * cap
        sel = jnp.where(sel == slot, 1.0, 0.0).astype(jnp.bfloat16)
        return jnp.dot(sel, normed[...], preferred_element_type=jnp.float32).astype(jnp.bfloat16)

    def zcopy(r, p):
        part = 2 * r + p
        return remote(
            send.at[r - 1, pl.ds(p * half, half), :], members.at[0, pl.ds(part * half, half), :],
            z_s.at[part], z_r.at[part], (peer[r], tile),
        )

    def spread(r, p):
        part = 2 * r + p
        line = pl.ds(part * half, half)
        src = members.at[0, line, :]
        copies = [
            remote(src, members.at[1, line, :], sib_s.at[part], sib_r.at[part], (me, sib)),
            remote(src, members.at[2, line, :], near_s.at[0, part], near_r.at[0, part], (me, xdev)),
            remote(src, members.at[3, line, :], near_s.at[1, part], near_r.at[1, part], (me, ydev)),
        ]
        for copy in copies[::-1]:
            copy.start()
        return copies

    def relay(part, copies):
        copies[2].wait_recv()
        line = pl.ds(part * half, half)
        copy = remote(members.at[3, line, :], members.at[4, line, :], relay_s.at[part], relay_r.at[part], (me, sib))

        @pl.when(xpos == 0)
        def _():
            copy.start()

        return copy

    def relayed(copies, wait):
        @pl.when(xpos == 0)
        def _():
            for copy in copies:
                wait(copy)

    zcopies = {}

    def begin(r, p):
        zcopies[r, p] = zcopy(r, p)
        zcopies[r, p].start()

    send[1] = filled(peer[2])
    pl.semaphore_wait(barrier, len(partners))
    begin(2, 0)
    send[0] = filled(peer[1])
    begin(1, 0)
    members[0, 0:cap, :] = filled(me)
    spreads, relays = [spread(0, 0), spread(0, 1)], []
    send[2] = filled(peer[3])

    marks = jnp.where(belongs, (cluster + 1).astype(jnp.float32), 0.0).astype(jnp.bfloat16)
    marked = lax.dot_general(marks, at_rank, NT, preferred_element_type=jnp.float32)
    tag_out[...] = jnp.zeros(tag_out.shape, jnp.float32)
    ztags = []
    for r in range(4):
        tag_out[r, :, r * cap : (r + 1) * cap] = marked
        if r:
            copy = remote(tag_out.at[r], tag_in.at[r - 1], ztag_s.at[r - 1], ztag_r.at[r - 1], (peer[r], tile))
            copy.start()
            ztags.append(copy)

    zcopies[2, 0].wait_send()
    begin(2, 1)
    zcopies[1, 0].wait_send()
    begin(1, 1)

    for copy in ztags:
        copy.wait_recv()
    total = tag_out[0] + tag_in[0] + tag_in[1] + tag_in[2]
    tags[0] = jnp.sum(
        jnp.where(lax.broadcasted_iota(jnp.int32, (8, slots), 0) == me, total, 0.0), axis=0, keepdims=True
    )
    ptags = []
    for n, device in enumerate((sib, xdev, ydev, ydev + beside)):
        copy = remote(tags.at[0], tags.at[1 + n], ptag_s.at[n], ptag_r.at[n], (me, device))
        copy.start()
        ptags.append(copy)

    zcopies[1, 0].wait_recv()
    spreads.append(spread(1, 0))
    zcopies[2, 0].wait_recv()
    spreads.append(spread(2, 0))
    zcopies[2, 1].wait_send()
    begin(3, 0)
    zcopies[1, 1].wait_recv()
    spreads.append(spread(1, 1))
    zcopies[2, 1].wait_recv()
    spreads.append(spread(2, 1))
    parts = [0, 1, 2, 4, 3, 5, 6, 7]

    for copy in ptags:
        copy.wait_recv()
    best[...] = jnp.full(best.shape, -1.0, jnp.float32)
    for n in range(5):
        for i in range(groups):
            first = i * cap // 128 * 128
            lanes = lax.broadcasted_iota(jnp.int32, (cap, 256), 1) + (first - i * cap)
            wanted = lax.broadcasted_iota(jnp.int32, (cap, 256), 0)
            picked = jnp.sum(
                jnp.where(lanes == wanted, tags[n, :, first : first + 256], 0.0), axis=1, keepdims=True
            )
            picked = jnp.where(picked > 0.0, picked, -1.0)
            key_tags[n, i * cap : (i + 1) * cap, :] = jnp.broadcast_to(picked, (cap, 128))

    def compare(kblock, keys, qblock, queries, to, own=False):
        (k0, k1), (q0, q1) = keys, queries
        shape = (k1 - k0, q1 - q0)
        scores = lax.dot_general(
            members[kblock, k0:k1, :], members[qblock, q0:q1, :], NT, preferred_element_type=jnp.float32
        )
        allowed = key_tags[kblock, k0:k1, 0:1] == tags[qblock, :, q0:q1]
        if own:
            line = lax.broadcasted_iota(jnp.int32, shape, 0) + (k0 + (kblock + qblock) * 2 * slots)
            lane = lax.broadcasted_iota(jnp.int32, shape, 1) + q0
            allowed = allowed & (line != lane)
        found = jnp.max(jnp.where(allowed, scores, -1.0), axis=0, keepdims=True)
        best[to, :, q0:q1] = jnp.maximum(best[to, :, q0:q1], found)

    first, last, whole = (0, early), (early, slots), (0, slots)

    for copies in spreads[:6]:
        copies[0].wait_recv()

    @pl.loop(0, 2)
    def _(q):
        compare(0, first, q, first, q, own=True)

    zcopies[3, 0].wait_send()
    begin(3, 1)
    for n in (0, 1, 2, 3):
        relays.append(relay(parts[n], spreads[n]))
    zcopies[3, 0].wait_recv()
    spreads.append(spread(3, 0))
    for n in (4, 5):
        relays.append(relay(parts[n], spreads[n]))
    for copies in spreads[:6]:
        copies[1].wait_recv()

    @pl.loop(0, 4)
    def _(i):
        q = lax.rem(i, 2)
        compare(2 + i // 2, first, q, first, q)

    zcopies[3, 1].wait_recv()
    spreads.append(spread(3, 1))
    relayed(relays[:6], lambda copy: copy.wait_recv())

    @pl.loop(0, 2)
    def _(q):
        compare(cross + q * (2 - cross), first, 2 + q * (cross - 2), first, 2 + q)

    relays.append(relay(parts[6], spreads[6]))
    for copies in spreads[6:]:
        copies[0].wait_recv()

    @pl.loop(0, 6)
    def _(i):
        j = i // 2
        q = lax.rem(i, 2)
        compare(j + (j + 1) // 2, first, q, last, q, own=True)

    @pl.loop(0, 2)
    def _(q):
        compare(0, last, q, whole, q, own=True)

    relays.append(relay(parts[7], spreads[7]))
    for copies in spreads[6:]:
        copies[1].wait_recv()

    @pl.loop(0, 4)
    def _(i):
        q = lax.rem(i, 2)
        compare(2 + i // 2, last, q, whole, q)

    relayed(relays[6:], lambda copy: copy.wait_recv())

    @pl.loop(0, 2)
    def _(q):
        compare(cross + q * (2 - cross), first, 2 + q * (cross - 2), last, 2 + q)

    @pl.loop(0, 2)
    def _(q):
        compare(cross + q * (2 - cross), last, 2 + q * (cross - 2), whole, 2 + q)

    copies = []
    for h, device in enumerate((tile, sib, xdev, crossdev)):
        for r in (3, 2, 1, 0):
            index = h * 4 + r
            if index == 0:
                result_in[0] = best[0]
                continue
            copy = remote(
                best.at[h], result_in.at[index], res_s.at[index], res_r.at[index], (peer[r], device)
            )
            copy.start()
            copies.append(copy)
    for copy in copies:
        copy.wait_recv()

    picks[...] = jnp.zeros(picks.shape, jnp.float32)
    for r in range(4):
        block = jnp.maximum(
            jnp.maximum(result_in[r], result_in[4 + r]), jnp.maximum(result_in[8 + r], result_in[12 + r])
        )[:, r * cap : (r + 1) * cap]
        high = block.astype(jnp.bfloat16).astype(jnp.float32)
        middle = (block - high).astype(jnp.bfloat16).astype(jnp.float32)
        picks[r : r + 1, :] = high
        picks[4 + r : 5 + r, :] = middle
        picks[8 + r : 9 + r, :] = (block - high) - middle
    found = jnp.dot(picks[...].astype(jnp.bfloat16), at_rank, preferred_element_type=jnp.float32)
    out = jnp.zeros((1, rows), jnp.float32)
    for r in range(4):
        value = (found[r : r + 1, :] + found[4 + r : 5 + r, :]) + found[8 + r : 9 + r, :]
        out = jnp.where(owner == peer[r], value, out)
    out_ref[...] = out.reshape(rows)

    for copy in ztags + ptags + copies + [zcopies[1, 1], zcopies[3, 1]]:
        copy.wait_send()
    for group in spreads:
        for copy in group:
            copy.wait_send()
    relayed(relays, lambda copy: copy.wait_send())


def local_fused(embeddings, row_group, row_cluster):
    rows, columns = embeddings.shape
    slots = 2 * rows
    dma = pltpu.SemaphoreType.DMA
    return pl.pallas_call(
        kernel,
        out_shape=jax.ShapeDtypeStruct((rows,), jnp.float32),
        in_specs=[pl.BlockSpec(memory_space=pltpu.HBM)] * 3,
        out_specs=pl.BlockSpec(memory_space=pltpu.VMEM),
        scratch_shapes=[
            pltpu.VMEM((rows, columns), jnp.bfloat16),
            pltpu.VMEM((rows,), jnp.int32),
            pltpu.VMEM((rows,), jnp.int32),
            pltpu.VMEM((rows, columns), jnp.bfloat16),
            pltpu.VMEM((3, slots // 4, columns), jnp.bfloat16),
            pltpu.VMEM((5, slots, columns), jnp.bfloat16),
            pltpu.VMEM((4, 8, slots), jnp.float32),
            pltpu.VMEM((3, 8, slots), jnp.float32),
            pltpu.VMEM((5, 1, slots), jnp.float32),
            pltpu.VMEM((5, slots, 128), jnp.float32),
            pltpu.VMEM((4, 1, slots), jnp.float32),
            pltpu.VMEM((16, 1, slots), jnp.float32),
            pltpu.VMEM((16, slots // 4), jnp.float32),
            dma((3,)),
            dma((3,)), dma((3,)), dma((8,)), dma((8,)),
            dma((4,)), dma((4,)), dma((8,)), dma((8,)),
            dma((2, 8)), dma((2, 8)), dma((8,)), dma((8,)),
            dma((16,)), dma((16,)),
        ],
        compiler_params=pltpu.CompilerParams(
            collective_id=0, has_side_effects=True, vmem_limit_bytes=64 * 1024 * 1024 - 256 * 1024
        ),
    )(embeddings, row_group, row_cluster)


def solution(mesh):
    fused = mesh.shape["grp"] == 4 and mesh.shape["tile"] == 8
    placed = (P(("grp", "tile"), None), P(("grp", "tile")), P(("grp", "tile")))
    return jax.shard_map(
        local_fused if fused else local_general,
        mesh=mesh, in_specs=placed, out_specs=P(("grp", "tile")), check_vma=False,
    )
```

```python
import jax
import jax.numpy as jnp
from jax import lax
from jax.experimental import pallas as pl
from jax.experimental.pallas import tpu as pltpu
from jax.sharding import PartitionSpec as P

MESH = pl.DeviceIdType.MESH
epsilon = 1e-06
NT = (((1,), (1,)), ((), ()))


def unit_rows(values):
    floats = values.astype(jnp.float32)
    scaled = floats * lax.rsqrt(jnp.sum(floats * floats, axis=-1, keepdims=True) + epsilon)
    return scaled.astype(jnp.bfloat16)


def slot_index(owners, groups, capacity):
    onehot = (owners[:, None] == jnp.arange(groups, dtype=jnp.int32)[None, :]).astype(jnp.int32)
    earlier = jnp.cumsum(onehot, axis=0) - onehot
    ranked = jnp.sum(earlier * onehot, axis=1)
    return owners * capacity + ranked


def masked_table(scores, left_ids, right_ids, left_pos, right_pos):
    allowed = (
        (left_ids[:, None] == right_ids[None, :])
        & (right_ids[None, :] >= 0)
        & (left_pos[:, None] != right_pos[None, :])
    )
    return jnp.where(allowed, scores, jnp.float32(-1.0))


def local_general(embeddings, row_group, row_cluster):
    row_count = embeddings.shape[0]
    columns = embeddings.shape[1]
    groups = lax.axis_size("grp")
    capacity = 2 * row_count // groups
    slots_all = groups * capacity
    placed = slot_index(row_group, groups, capacity)
    normed = unit_rows(embeddings)
    outgoing = (
        jnp.zeros((slots_all, columns), jnp.bfloat16)
        .at[placed]
        .set(normed)
        .reshape(groups, capacity, columns)
    )
    out_tags = (
        jnp.full((slots_all,), -1, jnp.int32).at[placed].set(row_cluster).reshape(groups, capacity)
    )
    members, member_ids = (
        lax.all_to_all(outgoing, "grp", split_axis=0, concat_axis=0, tiled=True),
        lax.all_to_all(out_tags, "grp", split_axis=0, concat_axis=0, tiled=True),
    )
    members = members.reshape(slots_all, columns)
    member_ids = member_ids.reshape(slots_all)
    tile_here = lax.axis_index("tile")
    local_pos = jnp.arange(slots_all, dtype=jnp.int32)
    own_pos = tile_here * slots_all + local_pos
    start_best = jnp.full((slots_all,), -1.0, jnp.float32)
    piece_rows = lax.all_gather(members, "tile", axis=0, tiled=True)
    piece_ids = lax.all_gather(member_ids, "tile", axis=0, tiled=True)
    scores = jnp.einsum("id,jd->ij", members, piece_rows, preferred_element_type=jnp.float32)
    piece_pos = jnp.arange(piece_rows.shape[0], dtype=jnp.int32)
    best_sim = jnp.maximum(
        start_best, jnp.max(masked_table(scores, member_ids, piece_ids, own_pos, piece_pos), axis=1)
    )
    results = best_sim.reshape(groups, capacity)
    arrived = lax.all_to_all(results, "grp", split_axis=0, concat_axis=0, tiled=True)
    return jnp.take(arrived.reshape(slots_all), placed)


def kernel(
    x_ref, owner_ref, cluster_ref, out_ref,
    loaded, owners, clusters, normed, send, members, tag_out, tag_in, tags, key_tags, best, result_in, picks, load_s,
    ztag_s, ztag_r, z_s, z_r, ptag_s, ptag_r, sib_s, sib_r, near_s, near_r, relay_s, relay_r, res_s, res_r,
):
    rows = x_ref.shape[0]
    groups = 4
    cap = 2 * rows // groups
    slots = groups * cap
    half = cap // 2
    early = 3 * cap
    me = lax.axis_index("grp")
    tile = lax.axis_index("tile")
    core = lax.rem(tile, 2)
    xpos = lax.rem(tile // 2, 2)
    ypos = tile // 4
    beside = 1 - 2 * core
    sib = tile + beside
    xdev = tile + 2 - 4 * xpos
    ydev = tile + 4 - 8 * ypos
    cross = 4 - xpos
    crossdev = ydev + (1 - xpos) * beside
    peer = (me, me + 1 - 2 * lax.rem(me, 2), me + 2 - 4 * (me // 2), 3 - me)

    partners = [(peer[r], tile) for r in (1, 2, 3)]
    partners += [(peer[r], device) for r in range(4) for device in (sib, xdev, ydev, ydev + beside)]
    barrier = pltpu.get_barrier_semaphore()
    for partner in partners:
        pl.semaphore_signal(barrier, inc=1, device_id=partner, device_id_type=MESH)

    loads = [
        pltpu.make_async_copy(src, dst, load_s.at[n])
        for n, (src, dst) in enumerate(((owner_ref, owners), (cluster_ref, clusters), (x_ref, loaded)))
    ]
    for load in loads:
        load.start()

    def remote(src, dst, ssem, rsem, device):
        return pltpu.make_async_remote_copy(
            src_ref=src, dst_ref=dst, send_sem=ssem, recv_sem=rsem, device_id=device, device_id_type=MESH
        )

    loads[0].wait()
    loads[1].wait()
    owner = owners[...].reshape(1, rows)
    cluster = clusters[...].reshape(1, rows)
    group_of = lax.broadcasted_iota(jnp.int32, (8, rows), 0)
    belongs = group_of == owner
    before = lax.broadcasted_iota(jnp.int32, (rows, rows), 0) < lax.broadcasted_iota(jnp.int32, (rows, rows), 1)
    earlier = jnp.dot(
        jnp.where(belongs, 1.0, 0.0).astype(jnp.bfloat16),
        jnp.where(before, 1.0, 0.0).astype(jnp.bfloat16),
        preferred_element_type=jnp.float32,
    )
    rank = jnp.sum(jnp.where(belongs, earlier, 0.0), axis=0, keepdims=True).astype(jnp.int32)
    slot = owner * cap + rank
    at_rank = jnp.where(lax.broadcasted_iota(jnp.int32, (cap, rows), 0) == rank, 1.0, 0.0).astype(jnp.bfloat16)

    loads[2].wait()
    chunk = rows // 4
    for c in range(4):
        part = pl.ds(c * chunk, chunk)
        normed[part, :] = unit_rows(loaded[part, :])

    def filled(group):
        sel = lax.broadcasted_iota(jnp.int32, (cap, rows), 0) + group * cap
        sel = jnp.where(sel == slot, 1.0, 0.0).astype(jnp.bfloat16)
        return jnp.dot(sel, normed[...], preferred_element_type=jnp.float32).astype(jnp.bfloat16)

    sixth = cap // 6
    parts = ((0, 0, 6), (1, 0, 3), (1, 3, 6), (2, 0, 1), (2, 1, 3), (2, 3, 6), (3, 0, 3), (3, 3, 6))

    def begin(part):
        r, low, high = parts[part]
        copy = remote(
            send.at[r - 1, pl.ds(low * sixth, (high - low) * sixth), :],
            members.at[0, pl.ds(r * cap + low * sixth, (high - low) * sixth), :],
            z_s.at[part], z_r.at[part], (peer[r], tile),
        )
        copy.start()
        zcopies[part] = copy

    def line_of(part):
        r, low, high = parts[part]
        return pl.ds(r * cap + low * sixth, (high - low) * sixth)

    def spread(part):
        if part:
            zcopies[part].wait_recv()
        line = line_of(part)
        src = members.at[0, line, :]
        copies = [
            remote(src, members.at[1, line, :], sib_s.at[part], sib_r.at[part], (me, sib)),
            remote(src, members.at[2, line, :], near_s.at[0, part], near_r.at[0, part], (me, xdev)),
            remote(src, members.at[3, line, :], near_s.at[1, part], near_r.at[1, part], (me, ydev)),
        ]
        for copy in copies[::-1]:
            copy.start()
        spreads[part] = copies

    def relay(part):
        spreads[part][2].wait_recv()
        line = line_of(part)
        copy = remote(members.at[3, line, :], members.at[4, line, :], relay_s.at[part], relay_r.at[part], (me, sib))

        @pl.when(xpos == 0)
        def _():
            copy.start()

        relays[part] = copy

    def relayed(copies, wait):
        @pl.when(xpos == 0)
        def _():
            for copy in copies:
                wait(copy)

    zcopies, spreads, relays = {}, {}, {}
    send[1] = filled(peer[2])
    pl.semaphore_wait(barrier, len(partners))
    begin(3)
    begin(4)
    send[0] = filled(peer[1])
    begin(1)
    members[0, 0:cap, :] = filled(me)
    spread(0)
    send[2] = filled(peer[3])

    marks = jnp.where(belongs, (cluster + 1).astype(jnp.float32), 0.0).astype(jnp.bfloat16)
    marked = lax.dot_general(marks, at_rank, NT, preferred_element_type=jnp.float32)
    tag_out[...] = jnp.zeros(tag_out.shape, jnp.float32)
    ztags = []
    for r in range(4):
        tag_out[r, :, r * cap : (r + 1) * cap] = marked
        if r:
            copy = remote(tag_out.at[r], tag_in.at[r - 1], ztag_s.at[r - 1], ztag_r.at[r - 1], (peer[r], tile))
            copy.start()
            ztags.append(copy)

    zcopies[3].wait_send()
    begin(5)
    spread(3)
    zcopies[1].wait_send()
    begin(2)
    spread(1)
    zcopies[4].wait_send()
    begin(6)
    spread(4)

    for copy in ztags:
        copy.wait_recv()
    total = tag_out[0] + tag_in[0] + tag_in[1] + tag_in[2]
    tags[0] = jnp.sum(
        jnp.where(lax.broadcasted_iota(jnp.int32, (8, slots), 0) == me, total, 0.0), axis=0, keepdims=True
    )
    ptags = []
    for n, device in enumerate((sib, xdev, ydev, ydev + beside)):
        copy = remote(tags.at[0], tags.at[1 + n], ptag_s.at[n], ptag_r.at[n], (me, device))
        copy.start()
        ptags.append(copy)

    for copy in ptags:
        copy.wait_recv()
    best[...] = jnp.full(best.shape, -1.0, jnp.float32)
    for n in range(5):
        for i in range(groups):
            first = i * cap // 128 * 128
            lanes = lax.broadcasted_iota(jnp.int32, (cap, 256), 1) + (first - i * cap)
            wanted = lax.broadcasted_iota(jnp.int32, (cap, 256), 0)
            picked = jnp.sum(
                jnp.where(lanes == wanted, tags[n, :, first : first + 256], 0.0), axis=1, keepdims=True
            )
            picked = jnp.where(picked > 0.0, picked, -1.0)
            key_tags[n, i * cap : (i + 1) * cap, :] = jnp.broadcast_to(picked, (cap, 128))

    def compare(kblock, keys, qblock, queries, to, own=False):
        (k0, k1), (q0, q1) = keys, queries
        shape = (k1 - k0, q1 - q0)
        scores = lax.dot_general(
            members[kblock, k0:k1, :], members[qblock, q0:q1, :], NT, preferred_element_type=jnp.float32
        )
        allowed = key_tags[kblock, k0:k1, 0:1] == tags[qblock, :, q0:q1]
        if own:
            line = lax.broadcasted_iota(jnp.int32, shape, 0) + (k0 + (kblock + qblock) * 2 * slots)
            lane = lax.broadcasted_iota(jnp.int32, shape, 1) + q0
            allowed = allowed & (line != lane)
        found = jnp.max(jnp.where(allowed, scores, -1.0), axis=0, keepdims=True)
        best[to, :, q0:q1] = jnp.maximum(best[to, :, q0:q1], found)

    first, last, whole = (0, early), (early, slots), (0, slots)

    spread(2)
    zcopies[5].wait_send()
    begin(7)
    spread(5)
    for part in range(6):
        spreads[part][0].wait_recv()

    @pl.loop(0, 2)
    def _(q):
        compare(0, first, q, first, q, own=True)

    for part in (0, 3, 1, 4, 2):
        relay(part)
    spread(6)
    relay(5)
    for part in range(6):
        spreads[part][1].wait_recv()

    @pl.loop(0, 4)
    def _(i):
        q = lax.rem(i, 2)
        compare(2 + i // 2, first, q, first, q)

    spread(7)
    relayed([relays[part] for part in range(6)], lambda copy: copy.wait_recv())

    @pl.loop(0, 2)
    def _(q):
        compare(cross + q * (2 - cross), first, 2 + q * (cross - 2), first, 2 + q)

    relay(6)
    for part in (6, 7):
        spreads[part][0].wait_recv()

    @pl.loop(0, 6)
    def _(i):
        j = i // 2
        q = lax.rem(i, 2)
        compare(j + (j + 1) // 2, first, q, last, q, own=True)

    @pl.loop(0, 2)
    def _(q):
        compare(0, last, q, whole, q, own=True)

    relay(7)
    for part in (6, 7):
        spreads[part][1].wait_recv()

    @pl.loop(0, 4)
    def _(i):
        q = lax.rem(i, 2)
        compare(2 + i // 2, last, q, whole, q)

    relayed([relays[6], relays[7]], lambda copy: copy.wait_recv())

    @pl.loop(0, 2)
    def _(q):
        compare(cross + q * (2 - cross), first, 2 + q * (cross - 2), last, 2 + q)

    @pl.loop(0, 2)
    def _(q):
        compare(cross + q * (2 - cross), last, 2 + q * (cross - 2), whole, 2 + q)

    copies = []
    for h, device in enumerate((tile, sib, xdev, crossdev)):
        for r in (3, 2, 1, 0):
            index = h * 4 + r
            if index == 0:
                result_in[0] = best[0]
                continue
            copy = remote(
                best.at[h], result_in.at[index], res_s.at[index], res_r.at[index], (peer[r], device)
            )
            copy.start()
            copies.append(copy)
    for copy in copies:
        copy.wait_recv()

    picks[...] = jnp.zeros(picks.shape, jnp.float32)
    for r in range(4):
        block = jnp.maximum(
            jnp.maximum(result_in[r], result_in[4 + r]), jnp.maximum(result_in[8 + r], result_in[12 + r])
        )[:, r * cap : (r + 1) * cap]
        high = block.astype(jnp.bfloat16).astype(jnp.float32)
        middle = (block - high).astype(jnp.bfloat16).astype(jnp.float32)
        picks[r : r + 1, :] = high
        picks[4 + r : 5 + r, :] = middle
        picks[8 + r : 9 + r, :] = (block - high) - middle
    found = jnp.dot(picks[...].astype(jnp.bfloat16), at_rank, preferred_element_type=jnp.float32)
    out = jnp.zeros((1, rows), jnp.float32)
    for r in range(4):
        value = (found[r : r + 1, :] + found[4 + r : 5 + r, :]) + found[8 + r : 9 + r, :]
        out = jnp.where(owner == peer[r], value, out)
    out_ref[...] = out.reshape(rows)

    for copy in ztags + ptags + copies + [zcopies[2], zcopies[6], zcopies[7]]:
        copy.wait_send()
    for group in spreads.values():
        for copy in group:
            copy.wait_send()
    relayed(list(relays.values()), lambda copy: copy.wait_send())


def local_fused(embeddings, row_group, row_cluster):
    rows, columns = embeddings.shape
    slots = 2 * rows
    dma = pltpu.SemaphoreType.DMA
    return pl.pallas_call(
        kernel,
        out_shape=jax.ShapeDtypeStruct((rows,), jnp.float32),
        in_specs=[pl.BlockSpec(memory_space=pltpu.HBM)] * 3,
        out_specs=pl.BlockSpec(memory_space=pltpu.VMEM),
        scratch_shapes=[
            pltpu.VMEM((rows, columns), jnp.bfloat16),
            pltpu.VMEM((rows,), jnp.int32),
            pltpu.VMEM((rows,), jnp.int32),
            pltpu.VMEM((rows, columns), jnp.bfloat16),
            pltpu.VMEM((3, slots // 4, columns), jnp.bfloat16),
            pltpu.VMEM((5, slots, columns), jnp.bfloat16),
            pltpu.VMEM((4, 8, slots), jnp.float32),
            pltpu.VMEM((3, 8, slots), jnp.float32),
            pltpu.VMEM((5, 1, slots), jnp.float32),
            pltpu.VMEM((5, slots, 128), jnp.float32),
            pltpu.VMEM((4, 1, slots), jnp.float32),
            pltpu.VMEM((16, 1, slots), jnp.float32),
            pltpu.VMEM((16, slots // 4), jnp.float32),
            dma((3,)),
            dma((3,)), dma((3,)), dma((8,)), dma((8,)),
            dma((4,)), dma((4,)), dma((8,)), dma((8,)),
            dma((2, 8)), dma((2, 8)), dma((8,)), dma((8,)),
            dma((16,)), dma((16,)),
        ],
        compiler_params=pltpu.CompilerParams(
            collective_id=0, has_side_effects=True, vmem_limit_bytes=64 * 1024 * 1024 - 256 * 1024
        ),
    )(embeddings, row_group, row_cluster)


def solution(mesh):
    fused = mesh.shape["grp"] == 4 and mesh.shape["tile"] == 8
    placed = (P(("grp", "tile"), None), P(("grp", "tile")), P(("grp", "tile")))
    return jax.shard_map(
        local_fused if fused else local_general,
        mesh=mesh, in_specs=placed, out_specs=P(("grp", "tile")), check_vma=False,
    )
```

```python
import jax
import jax.numpy as jnp
from jax import lax
from jax.experimental import pallas as pl
from jax.experimental.pallas import tpu as pltpu
from jax.sharding import PartitionSpec as P

MESH = pl.DeviceIdType.MESH
epsilon = 1e-06
NT = (((1,), (1,)), ((), ()))


def unit_rows(values):
    floats = values.astype(jnp.float32)
    scaled = floats * lax.rsqrt(jnp.sum(floats * floats, axis=-1, keepdims=True) + epsilon)
    return scaled.astype(jnp.bfloat16)


def slot_index(owners, groups, capacity):
    onehot = (owners[:, None] == jnp.arange(groups, dtype=jnp.int32)[None, :]).astype(jnp.int32)
    earlier = jnp.cumsum(onehot, axis=0) - onehot
    ranked = jnp.sum(earlier * onehot, axis=1)
    return owners * capacity + ranked


def masked_table(scores, left_ids, right_ids, left_pos, right_pos):
    allowed = (
        (left_ids[:, None] == right_ids[None, :])
        & (right_ids[None, :] >= 0)
        & (left_pos[:, None] != right_pos[None, :])
    )
    return jnp.where(allowed, scores, jnp.float32(-1.0))


def local_general(embeddings, row_group, row_cluster):
    row_count = embeddings.shape[0]
    columns = embeddings.shape[1]
    groups = lax.axis_size("grp")
    capacity = 2 * row_count // groups
    slots_all = groups * capacity
    placed = slot_index(row_group, groups, capacity)
    normed = unit_rows(embeddings)
    outgoing = (
        jnp.zeros((slots_all, columns), jnp.bfloat16)
        .at[placed]
        .set(normed)
        .reshape(groups, capacity, columns)
    )
    out_tags = (
        jnp.full((slots_all,), -1, jnp.int32).at[placed].set(row_cluster).reshape(groups, capacity)
    )
    members, member_ids = (
        lax.all_to_all(outgoing, "grp", split_axis=0, concat_axis=0, tiled=True),
        lax.all_to_all(out_tags, "grp", split_axis=0, concat_axis=0, tiled=True),
    )
    members = members.reshape(slots_all, columns)
    member_ids = member_ids.reshape(slots_all)
    tile_here = lax.axis_index("tile")
    local_pos = jnp.arange(slots_all, dtype=jnp.int32)
    own_pos = tile_here * slots_all + local_pos
    start_best = jnp.full((slots_all,), -1.0, jnp.float32)
    piece_rows = lax.all_gather(members, "tile", axis=0, tiled=True)
    piece_ids = lax.all_gather(member_ids, "tile", axis=0, tiled=True)
    scores = jnp.einsum("id,jd->ij", members, piece_rows, preferred_element_type=jnp.float32)
    piece_pos = jnp.arange(piece_rows.shape[0], dtype=jnp.int32)
    best_sim = jnp.maximum(
        start_best, jnp.max(masked_table(scores, member_ids, piece_ids, own_pos, piece_pos), axis=1)
    )
    results = best_sim.reshape(groups, capacity)
    arrived = lax.all_to_all(results, "grp", split_axis=0, concat_axis=0, tiled=True)
    return jnp.take(arrived.reshape(slots_all), placed)


def kernel(
    x_ref, owner_ref, cluster_ref, out_ref,
    loaded, owners, clusters, normed, send, members, tag_out, tag_in, tags, key_tags, best, key_best, result_in, picks, load_s,
    ztag_s, ztag_r, z_s, z_r, ptag_s, ptag_r, sib_s, sib_r, near_s, near_r, relay_s, relay_r, res_s, res_r,
):
    rows = x_ref.shape[0]
    groups = 4
    cap = 2 * rows // groups
    slots = groups * cap
    half = cap // 2
    early = 3 * cap
    me = lax.axis_index("grp")
    tile = lax.axis_index("tile")
    core = lax.rem(tile, 2)
    xpos = lax.rem(tile // 2, 2)
    ypos = tile // 4
    beside = 1 - 2 * core
    sib = tile + beside
    xdev = tile + 2 - 4 * xpos
    ydev = tile + 4 - 8 * ypos
    cross = 4 - xpos
    crossdev = ydev + (1 - xpos) * beside
    peer = (me, me + 1 - 2 * lax.rem(me, 2), me + 2 - 4 * (me // 2), 3 - me)

    partners = [(peer[r], tile) for r in (1, 2, 3)]
    partners += [(peer[r], device) for r in range(4) for device in (sib, xdev, ydev, ydev + beside)]
    barrier = pltpu.get_barrier_semaphore()
    for partner in partners:
        pl.semaphore_signal(barrier, inc=1, device_id=partner, device_id_type=MESH)

    loads = [
        pltpu.make_async_copy(src, dst, load_s.at[n])
        for n, (src, dst) in enumerate(((owner_ref, owners), (cluster_ref, clusters), (x_ref, loaded)))
    ]
    for load in loads:
        load.start()

    def remote(src, dst, ssem, rsem, device):
        return pltpu.make_async_remote_copy(
            src_ref=src, dst_ref=dst, send_sem=ssem, recv_sem=rsem, device_id=device, device_id_type=MESH
        )

    loads[0].wait()
    loads[1].wait()
    owner = owners[...].reshape(1, rows)
    cluster = clusters[...].reshape(1, rows)
    group_of = lax.broadcasted_iota(jnp.int32, (8, rows), 0)
    belongs = group_of == owner
    before = lax.broadcasted_iota(jnp.int32, (rows, rows), 0) < lax.broadcasted_iota(jnp.int32, (rows, rows), 1)
    earlier = jnp.dot(
        jnp.where(belongs, 1.0, 0.0).astype(jnp.bfloat16),
        jnp.where(before, 1.0, 0.0).astype(jnp.bfloat16),
        preferred_element_type=jnp.float32,
    )
    rank = jnp.sum(jnp.where(belongs, earlier, 0.0), axis=0, keepdims=True).astype(jnp.int32)
    slot = owner * cap + rank
    at_rank = jnp.where(lax.broadcasted_iota(jnp.int32, (cap, rows), 0) == rank, 1.0, 0.0).astype(jnp.bfloat16)

    loads[2].wait()
    chunk = rows // 4
    for c in range(4):
        part = pl.ds(c * chunk, chunk)
        normed[part, :] = unit_rows(loaded[part, :])

    def filled(group):
        sel = lax.broadcasted_iota(jnp.int32, (cap, rows), 0) + group * cap
        sel = jnp.where(sel == slot, 1.0, 0.0).astype(jnp.bfloat16)
        return jnp.dot(sel, normed[...], preferred_element_type=jnp.float32).astype(jnp.bfloat16)

    sixth = cap // 6
    parts = ((0, 0, 6), (1, 0, 3), (1, 3, 6), (2, 0, 1), (2, 1, 3), (2, 3, 6), (3, 0, 3), (3, 3, 6))

    def begin(part):
        r, low, high = parts[part]
        copy = remote(
            send.at[r - 1, pl.ds(low * sixth, (high - low) * sixth), :],
            members.at[0, pl.ds(r * cap + low * sixth, (high - low) * sixth), :],
            z_s.at[part], z_r.at[part], (peer[r], tile),
        )
        copy.start()
        zcopies[part] = copy

    def line_of(part):
        r, low, high = parts[part]
        return pl.ds(r * cap + low * sixth, (high - low) * sixth)

    def spread(part):
        if part:
            zcopies[part].wait_recv()
        line = line_of(part)
        src = members.at[0, line, :]
        copies = [
            remote(src, members.at[1, line, :], sib_s.at[part], sib_r.at[part], (me, sib)),
            remote(src, members.at[2, line, :], near_s.at[0, part], near_r.at[0, part], (me, xdev)),
            remote(src, members.at[3, line, :], near_s.at[1, part], near_r.at[1, part], (me, ydev)),
        ]
        for copy in copies[::-1]:
            copy.start()
        spreads[part] = copies

    def relay(part):
        spreads[part][2].wait_recv()
        line = line_of(part)
        copy = remote(members.at[3, line, :], members.at[4, line, :], relay_s.at[part], relay_r.at[part], (me, sib))

        @pl.when(xpos == 0)
        def _():
            copy.start()

        relays[part] = copy

    def relayed(copies, wait):
        @pl.when(xpos == 0)
        def _():
            for copy in copies:
                wait(copy)

    zcopies, spreads, relays = {}, {}, {}
    send[1] = filled(peer[2])
    pl.semaphore_wait(barrier, len(partners))
    begin(3)
    begin(4)
    send[0] = filled(peer[1])
    begin(1)
    members[0, 0:cap, :] = filled(me)
    spread(0)
    send[2] = filled(peer[3])

    marks = jnp.where(belongs, (cluster + 1).astype(jnp.float32), 0.0).astype(jnp.bfloat16)
    marked = lax.dot_general(marks, at_rank, NT, preferred_element_type=jnp.float32)
    tag_out[...] = jnp.zeros(tag_out.shape, jnp.float32)
    ztags = []
    for r in range(4):
        tag_out[r, :, r * cap : (r + 1) * cap] = marked
        if r:
            copy = remote(tag_out.at[r], tag_in.at[r - 1], ztag_s.at[r - 1], ztag_r.at[r - 1], (peer[r], tile))
            copy.start()
            ztags.append(copy)

    zcopies[3].wait_send()
    begin(5)
    spread(3)
    zcopies[1].wait_send()
    begin(2)
    spread(1)
    zcopies[4].wait_send()
    begin(6)
    spread(4)

    for copy in ztags:
        copy.wait_recv()
    total = tag_out[0] + tag_in[0] + tag_in[1] + tag_in[2]
    tags[0] = jnp.sum(
        jnp.where(lax.broadcasted_iota(jnp.int32, (8, slots), 0) == me, total, 0.0), axis=0, keepdims=True
    )
    ptags = []
    for n, device in enumerate((sib, xdev, ydev, ydev + beside)):
        copy = remote(tags.at[0], tags.at[1 + n], ptag_s.at[n], ptag_r.at[n], (me, device))
        copy.start()
        ptags.append(copy)

    for copy in ptags:
        copy.wait_recv()
    best[...] = jnp.full(best.shape, -1.0, jnp.float32)
    key_best[...] = jnp.full(key_best.shape, -1.0, jnp.float32)
    for n in range(5):
        for i in range(groups):
            first = i * cap // 128 * 128
            lanes = lax.broadcasted_iota(jnp.int32, (cap, 256), 1) + (first - i * cap)
            wanted = lax.broadcasted_iota(jnp.int32, (cap, 256), 0)
            picked = jnp.sum(
                jnp.where(lanes == wanted, tags[n, :, first : first + 256], 0.0), axis=1, keepdims=True
            )
            picked = jnp.where(picked > 0.0, picked, -1.0)
            key_tags[n, i * cap : (i + 1) * cap, :] = jnp.broadcast_to(picked, (cap, 128))

    def compare(kblock, keys, qblock, queries, to, own=False, back=None):
        (k0, k1), (q0, q1) = keys, queries
        shape = (k1 - k0, q1 - q0)
        scores = lax.dot_general(
            members[kblock, k0:k1, :], members[qblock, q0:q1, :], NT, preferred_element_type=jnp.float32
        )
        allowed = key_tags[kblock, k0:k1, 0:1] == tags[qblock, :, q0:q1]
        if own:
            line = lax.broadcasted_iota(jnp.int32, shape, 0) + (k0 + (kblock + qblock) * 2 * slots)
            lane = lax.broadcasted_iota(jnp.int32, shape, 1) + q0
            allowed = allowed & (line != lane)
        masked = jnp.where(allowed, scores, -1.0)
        found = jnp.max(masked, axis=0, keepdims=True)
        best[to, :, q0:q1] = jnp.maximum(best[to, :, q0:q1], found)
        if back is not None:
            full = shape[1] // 128 * 128
            across = key_best[back, k0:k1, :]
            for lane in range(0, full, 128):
                across = jnp.maximum(across, masked[:, lane : lane + 128])
            key_best[back, k0:k1, :] = across
            rest = shape[1] - full
            if rest:
                key_best[back, k0:k1, :rest] = jnp.maximum(key_best[back, k0:k1, :rest], masked[:, full:])

    first, last, whole = (0, early), (early, slots), (0, slots)

    spread(2)
    zcopies[5].wait_send()
    begin(7)
    spread(5)
    for part in range(6):
        spreads[part][0].wait_recv()

    @pl.loop(0, 2)
    def _(q):
        compare(0, first, q, first, q, own=True)

    for part in (0, 3, 1, 4, 2):
        relay(part)
    spread(6)
    relay(5)
    for part in range(6):
        spreads[part][1].wait_recv()

    def beside_block(i):
        return xpos + i * (ypos - xpos)

    @pl.loop(0, 2)
    def _(i):
        compare(2 + i, first, beside_block(i), first, beside_block(i), back=i)

    spread(7)
    relayed([relays[part] for part in range(6)], lambda copy: copy.wait_recv())

    compare(cross, first, 2, first, 2, back=2)

    relay(6)
    for part in (6, 7):
        spreads[part][0].wait_recv()

    @pl.loop(0, 2)
    def _(q):
        compare(0, first, q, last, q, own=True)

    @pl.loop(0, 2)
    def _(i):
        compare(2 + i, first, beside_block(i), last, beside_block(i), back=i)

    @pl.loop(0, 2)
    def _(q):
        compare(0, last, q, whole, q, own=True)

    relay(7)
    for part in (6, 7):
        spreads[part][1].wait_recv()

    @pl.loop(0, 2)
    def _(i):
        compare(2 + i, last, beside_block(i), whole, beside_block(i), back=i)

    relayed([relays[6], relays[7]], lambda copy: copy.wait_recv())

    compare(cross, first, 2, last, 2, back=2)
    compare(cross, last, 2, whole, 2, back=2)

    def turned(back):
        return jnp.max(key_best[back].T, axis=0, keepdims=True)

    best[2] = jnp.maximum(best[2], turned(0))
    best[3] = turned(2)
    best[4] = turned(1)

    copies = []
    for h, device in enumerate((tile, sib, xdev, crossdev, ydev)):
        for r in (3, 2, 1, 0):
            index = h * 4 + r
            if index == 0:
                result_in[0] = best[0]
                continue
            copy = remote(
                best.at[h], result_in.at[index], res_s.at[index], res_r.at[index], (peer[r], device)
            )
            copy.start()
            copies.append(copy)
    for copy in copies:
        copy.wait_recv()

    picks[...] = jnp.zeros(picks.shape, jnp.float32)
    for r in range(4):
        block = jnp.maximum(
            jnp.maximum(result_in[r], result_in[4 + r]), jnp.maximum(result_in[8 + r], result_in[12 + r])
        )
        block = jnp.maximum(block, result_in[16 + r])[:, r * cap : (r + 1) * cap]
        high = block.astype(jnp.bfloat16).astype(jnp.float32)
        middle = (block - high).astype(jnp.bfloat16).astype(jnp.float32)
        picks[r : r + 1, :] = high
        picks[4 + r : 5 + r, :] = middle
        picks[8 + r : 9 + r, :] = (block - high) - middle
    found = jnp.dot(picks[...].astype(jnp.bfloat16), at_rank, preferred_element_type=jnp.float32)
    out = jnp.zeros((1, rows), jnp.float32)
    for r in range(4):
        value = (found[r : r + 1, :] + found[4 + r : 5 + r, :]) + found[8 + r : 9 + r, :]
        out = jnp.where(owner == peer[r], value, out)
    out_ref[...] = out.reshape(rows)

    for copy in ztags + ptags + copies + [zcopies[2], zcopies[6], zcopies[7]]:
        copy.wait_send()
    for group in spreads.values():
        for copy in group:
            copy.wait_send()
    relayed(list(relays.values()), lambda copy: copy.wait_send())


def local_fused(embeddings, row_group, row_cluster):
    rows, columns = embeddings.shape
    slots = 2 * rows
    dma = pltpu.SemaphoreType.DMA
    return pl.pallas_call(
        kernel,
        out_shape=jax.ShapeDtypeStruct((rows,), jnp.float32),
        in_specs=[pl.BlockSpec(memory_space=pltpu.HBM)] * 3,
        out_specs=pl.BlockSpec(memory_space=pltpu.VMEM),
        scratch_shapes=[
            pltpu.VMEM((rows, columns), jnp.bfloat16),
            pltpu.VMEM((rows,), jnp.int32),
            pltpu.VMEM((rows,), jnp.int32),
            pltpu.VMEM((rows, columns), jnp.bfloat16),
            pltpu.VMEM((3, slots // 4, columns), jnp.bfloat16),
            pltpu.VMEM((5, slots, columns), jnp.bfloat16),
            pltpu.VMEM((4, 8, slots), jnp.float32),
            pltpu.VMEM((3, 8, slots), jnp.float32),
            pltpu.VMEM((5, 1, slots), jnp.float32),
            pltpu.VMEM((5, slots, 128), jnp.float32),
            pltpu.VMEM((5, 1, slots), jnp.float32),
            pltpu.VMEM((3, slots, 128), jnp.float32),
            pltpu.VMEM((20, 1, slots), jnp.float32),
            pltpu.VMEM((16, slots // 4), jnp.float32),
            dma((3,)),
            dma((3,)), dma((3,)), dma((8,)), dma((8,)),
            dma((4,)), dma((4,)), dma((8,)), dma((8,)),
            dma((2, 8)), dma((2, 8)), dma((8,)), dma((8,)),
            dma((20,)), dma((20,)),
        ],
        compiler_params=pltpu.CompilerParams(
            collective_id=0, has_side_effects=True, vmem_limit_bytes=64 * 1024 * 1024 - 256 * 1024
        ),
    )(embeddings, row_group, row_cluster)


def solution(mesh):
    fused = mesh.shape["grp"] == 4 and mesh.shape["tile"] == 8
    placed = (P(("grp", "tile"), None), P(("grp", "tile")), P(("grp", "tile")))
    return jax.shard_map(
        local_fused if fused else local_general,
        mesh=mesh, in_specs=placed, out_specs=P(("grp", "tile")), check_vma=False,
    )
```

```python
import jax
import jax.numpy as jnp
from jax import lax
from jax.experimental import pallas as pl
from jax.experimental.pallas import tpu as pltpu
from jax.sharding import PartitionSpec as P

MESH = pl.DeviceIdType.MESH
epsilon = 1e-06
NT = (((1,), (1,)), ((), ()))


def unit_rows(values):
    floats = values.astype(jnp.float32)
    scaled = floats * lax.rsqrt(jnp.sum(floats * floats, axis=-1, keepdims=True) + epsilon)
    return scaled.astype(jnp.bfloat16)


def slot_index(owners, groups, capacity):
    onehot = (owners[:, None] == jnp.arange(groups, dtype=jnp.int32)[None, :]).astype(jnp.int32)
    earlier = jnp.cumsum(onehot, axis=0) - onehot
    ranked = jnp.sum(earlier * onehot, axis=1)
    return owners * capacity + ranked


def masked_table(scores, left_ids, right_ids, left_pos, right_pos):
    allowed = (
        (left_ids[:, None] == right_ids[None, :])
        & (right_ids[None, :] >= 0)
        & (left_pos[:, None] != right_pos[None, :])
    )
    return jnp.where(allowed, scores, jnp.float32(-1.0))


def local_general(embeddings, row_group, row_cluster):
    row_count = embeddings.shape[0]
    columns = embeddings.shape[1]
    groups = lax.axis_size("grp")
    capacity = 2 * row_count // groups
    slots_all = groups * capacity
    placed = slot_index(row_group, groups, capacity)
    normed = unit_rows(embeddings)
    outgoing = (
        jnp.zeros((slots_all, columns), jnp.bfloat16)
        .at[placed]
        .set(normed)
        .reshape(groups, capacity, columns)
    )
    out_tags = (
        jnp.full((slots_all,), -1, jnp.int32).at[placed].set(row_cluster).reshape(groups, capacity)
    )
    members, member_ids = (
        lax.all_to_all(outgoing, "grp", split_axis=0, concat_axis=0, tiled=True),
        lax.all_to_all(out_tags, "grp", split_axis=0, concat_axis=0, tiled=True),
    )
    members = members.reshape(slots_all, columns)
    member_ids = member_ids.reshape(slots_all)
    tile_here = lax.axis_index("tile")
    local_pos = jnp.arange(slots_all, dtype=jnp.int32)
    own_pos = tile_here * slots_all + local_pos
    start_best = jnp.full((slots_all,), -1.0, jnp.float32)
    piece_rows = lax.all_gather(members, "tile", axis=0, tiled=True)
    piece_ids = lax.all_gather(member_ids, "tile", axis=0, tiled=True)
    scores = jnp.einsum("id,jd->ij", members, piece_rows, preferred_element_type=jnp.float32)
    piece_pos = jnp.arange(piece_rows.shape[0], dtype=jnp.int32)
    best_sim = jnp.maximum(
        start_best, jnp.max(masked_table(scores, member_ids, piece_ids, own_pos, piece_pos), axis=1)
    )
    results = best_sim.reshape(groups, capacity)
    arrived = lax.all_to_all(results, "grp", split_axis=0, concat_axis=0, tiled=True)
    return jnp.take(arrived.reshape(slots_all), placed)


def kernel(
    x_ref, owner_ref, cluster_ref, out_ref,
    loaded, owners, clusters, normed, send, members, tag_out, tag_in, tags, key_tags, best, key_best, result_in, picks, load_s,
    ztag_s, ztag_r, z_s, z_r, ptag_s, ptag_r, sib_s, sib_r, near_s, near_r, relay_s, relay_r, res_s, res_r,
):
    rows = x_ref.shape[0]
    groups = 4
    cap = 2 * rows // groups
    slots = groups * cap
    half = cap // 2
    early = 3 * cap
    me = lax.axis_index("grp")
    tile = lax.axis_index("tile")
    core = lax.rem(tile, 2)
    xpos = lax.rem(tile // 2, 2)
    ypos = tile // 4
    beside = 1 - 2 * core
    sib = tile + beside
    xdev = tile + 2 - 4 * xpos
    ydev = tile + 4 - 8 * ypos
    cross = 4 - xpos
    crossdev = ydev + (1 - xpos) * beside
    peer = (me, me + 1 - 2 * lax.rem(me, 2), me + 2 - 4 * (me // 2), 3 - me)

    partners = [(peer[r], tile) for r in (1, 2, 3)]
    partners += [(peer[r], device) for r in range(4) for device in (sib, xdev, ydev, ydev + beside)]
    barrier = pltpu.get_barrier_semaphore()
    for partner in partners:
        pl.semaphore_signal(barrier, inc=1, device_id=partner, device_id_type=MESH)

    loads = [
        pltpu.make_async_copy(src, dst, load_s.at[n])
        for n, (src, dst) in enumerate(((owner_ref, owners), (cluster_ref, clusters), (x_ref, loaded)))
    ]
    for load in loads:
        load.start()

    def remote(src, dst, ssem, rsem, device):
        return pltpu.make_async_remote_copy(
            src_ref=src, dst_ref=dst, send_sem=ssem, recv_sem=rsem, device_id=device, device_id_type=MESH
        )

    loads[0].wait()
    loads[1].wait()
    owner = owners[...].reshape(1, rows)
    cluster = clusters[...].reshape(1, rows)
    group_of = lax.broadcasted_iota(jnp.int32, (8, rows), 0)
    belongs = group_of == owner
    before = lax.broadcasted_iota(jnp.int32, (rows, rows), 0) < lax.broadcasted_iota(jnp.int32, (rows, rows), 1)
    earlier = jnp.dot(
        jnp.where(belongs, 1.0, 0.0).astype(jnp.bfloat16),
        jnp.where(before, 1.0, 0.0).astype(jnp.bfloat16),
        preferred_element_type=jnp.float32,
    )
    rank = jnp.sum(jnp.where(belongs, earlier, 0.0), axis=0, keepdims=True).astype(jnp.int32)
    slot = owner * cap + rank
    at_rank = jnp.where(lax.broadcasted_iota(jnp.int32, (cap, rows), 0) == rank, 1.0, 0.0).astype(jnp.bfloat16)

    loads[2].wait()
    chunk = rows // 4
    for c in range(4):
        part = pl.ds(c * chunk, chunk)
        normed[part, :] = unit_rows(loaded[part, :])

    def filled(group):
        sel = lax.broadcasted_iota(jnp.int32, (cap, rows), 0) + group * cap
        sel = jnp.where(sel == slot, 1.0, 0.0).astype(jnp.bfloat16)
        return jnp.dot(sel, normed[...], preferred_element_type=jnp.float32).astype(jnp.bfloat16)

    sixth = cap // 6
    parts = ((0, 0, 6), (1, 0, 3), (1, 3, 6), (2, 0, 1), (2, 1, 3), (2, 3, 6), (3, 0, 3), (3, 3, 5), (3, 5, 6))

    def begin(part):
        r, low, high = parts[part]
        copy = remote(
            send.at[r - 1, pl.ds(low * sixth, (high - low) * sixth), :],
            members.at[0, pl.ds(r * cap + low * sixth, (high - low) * sixth), :],
            z_s.at[part], z_r.at[part], (peer[r], tile),
        )
        copy.start()
        zcopies[part] = copy

    def line_of(part):
        r, low, high = parts[part]
        return pl.ds(r * cap + low * sixth, (high - low) * sixth)

    def spread(part):
        if part:
            zcopies[part].wait_recv()
        line = line_of(part)
        src = members.at[0, line, :]
        copies = [
            remote(src, members.at[1, line, :], sib_s.at[part], sib_r.at[part], (me, sib)),
            remote(src, members.at[2, line, :], near_s.at[0, part], near_r.at[0, part], (me, xdev)),
            remote(src, members.at[3, line, :], near_s.at[1, part], near_r.at[1, part], (me, ydev)),
        ]
        for copy in copies[::-1]:
            copy.start()
        spreads[part] = copies

    def relay(part):
        spreads[part][2].wait_recv()
        line = line_of(part)
        copy = remote(members.at[3, line, :], members.at[4, line, :], relay_s.at[part], relay_r.at[part], (me, sib))

        @pl.when(xpos == 0)
        def _():
            copy.start()

        relays[part] = copy

    def relayed(copies, wait):
        @pl.when(xpos == 0)
        def _():
            for copy in copies:
                wait(copy)

    zcopies, spreads, relays = {}, {}, {}
    send[1] = filled(peer[2])
    pl.semaphore_wait(barrier, len(partners))
    begin(3)
    begin(4)
    send[0] = filled(peer[1])
    begin(1)
    members[0, 0:cap, :] = filled(me)
    spread(0)
    send[2] = filled(peer[3])

    marks = jnp.where(belongs, (cluster + 1).astype(jnp.float32), 0.0).astype(jnp.bfloat16)
    marked = lax.dot_general(marks, at_rank, NT, preferred_element_type=jnp.float32)
    tag_out[...] = jnp.zeros(tag_out.shape, jnp.float32)
    ztags = []
    for r in range(4):
        tag_out[r, :, r * cap : (r + 1) * cap] = marked
        if r:
            copy = remote(tag_out.at[r], tag_in.at[r - 1], ztag_s.at[r - 1], ztag_r.at[r - 1], (peer[r], tile))
            copy.start()
            ztags.append(copy)

    zcopies[3].wait_send()
    begin(5)
    spread(3)
    zcopies[1].wait_send()
    begin(2)
    spread(1)
    zcopies[4].wait_send()
    begin(6)
    spread(4)

    for copy in ztags:
        copy.wait_recv()
    total = tag_out[0] + tag_in[0] + tag_in[1] + tag_in[2]
    tags[0] = jnp.sum(
        jnp.where(lax.broadcasted_iota(jnp.int32, (8, slots), 0) == me, total, 0.0), axis=0, keepdims=True
    )
    ptags = []
    for n, device in enumerate((sib, xdev, ydev, ydev + beside)):
        copy = remote(tags.at[0], tags.at[1 + n], ptag_s.at[n], ptag_r.at[n], (me, device))
        copy.start()
        ptags.append(copy)

    for copy in ptags:
        copy.wait_recv()
    best[...] = jnp.full(best.shape, -1.0, jnp.float32)
    key_best[...] = jnp.full(key_best.shape, -1.0, jnp.float32)
    for n in range(5):
        for i in range(groups):
            first = i * cap // 128 * 128
            lanes = lax.broadcasted_iota(jnp.int32, (cap, 256), 1) + (first - i * cap)
            wanted = lax.broadcasted_iota(jnp.int32, (cap, 256), 0)
            picked = jnp.sum(
                jnp.where(lanes == wanted, tags[n, :, first : first + 256], 0.0), axis=1, keepdims=True
            )
            picked = jnp.where(picked > 0.0, picked, -1.0)
            key_tags[n, i * cap : (i + 1) * cap, :] = jnp.broadcast_to(picked, (cap, 128))

    def compare(kblock, keys, qblock, queries, to, own=False, back=None):
        (k0, k1), (q0, q1) = keys, queries
        shape = (k1 - k0, q1 - q0)
        scores = lax.dot_general(
            members[kblock, k0:k1, :], members[qblock, q0:q1, :], NT, preferred_element_type=jnp.float32
        )
        allowed = key_tags[kblock, k0:k1, 0:1] == tags[qblock, :, q0:q1]
        if own:
            line = lax.broadcasted_iota(jnp.int32, shape, 0) + (k0 + (kblock + qblock) * 2 * slots)
            lane = lax.broadcasted_iota(jnp.int32, shape, 1) + q0
            allowed = allowed & (line != lane)
        masked = jnp.where(allowed, scores, -1.0)
        found = jnp.max(masked, axis=0, keepdims=True)
        best[to, :, q0:q1] = jnp.maximum(best[to, :, q0:q1], found)
        if back is not None:
            full = shape[1] // 128 * 128
            across = key_best[back, k0:k1, :]
            for lane in range(0, full, 128):
                across = jnp.maximum(across, masked[:, lane : lane + 128])
            key_best[back, k0:k1, :] = across
            rest = shape[1] - full
            if rest:
                key_best[back, k0:k1, :rest] = jnp.maximum(key_best[back, k0:k1, :rest], masked[:, full:])

    first, last, whole = (0, early), (early, slots), (0, slots)

    spread(2)
    zcopies[5].wait_send()
    begin(7)
    spread(5)
    for part in range(6):
        spreads[part][0].wait_recv()

    @pl.loop(0, 2)
    def _(q):
        compare(0, first, q, first, q, own=True)

    for part in (0, 3, 1, 4, 2):
        relay(part)
    zcopies[6].wait_send()
    begin(8)
    spread(6)
    relay(5)
    for part in range(6):
        spreads[part][1].wait_recv()

    def beside_block(i):
        return xpos + i * (ypos - xpos)

    @pl.loop(0, 2)
    def _(i):
        compare(2 + i, first, beside_block(i), first, beside_block(i), back=i)

    spread(7)
    spread(8)
    relayed([relays[part] for part in range(6)], lambda copy: copy.wait_recv())

    compare(cross, first, 2, first, 2, back=2)

    relay(6)
    for part in (6, 7, 8):
        spreads[part][0].wait_recv()

    @pl.loop(0, 2)
    def _(q):
        compare(0, first, q, last, q, own=True)

    @pl.loop(0, 2)
    def _(i):
        compare(2 + i, first, beside_block(i), last, beside_block(i), back=i)

    @pl.loop(0, 2)
    def _(q):
        compare(0, last, q, whole, q, own=True)

    relay(7)
    relay(8)
    for part in (6, 7, 8):
        spreads[part][1].wait_recv()

    @pl.loop(0, 2)
    def _(i):
        compare(2 + i, last, beside_block(i), whole, beside_block(i), back=i)

    compare(cross, first, 2, last, 2, back=2)
    relayed([relays[part] for part in (6, 7, 8)], lambda copy: copy.wait_recv())
    compare(cross, last, 2, whole, 2, back=2)

    def turned(back):
        return jnp.max(key_best[back].T, axis=0, keepdims=True)

    best[2] = jnp.maximum(best[2], turned(0))
    best[3] = turned(2)
    best[4] = turned(1)

    copies = []
    for h, device in enumerate((tile, sib, xdev, crossdev, ydev)):
        for r in (3, 2, 1, 0):
            index = h * 4 + r
            if index == 0:
                result_in[0] = best[0]
                continue
            copy = remote(
                best.at[h], result_in.at[index], res_s.at[index], res_r.at[index], (peer[r], device)
            )
            copy.start()
            copies.append(copy)
    for copy in copies:
        copy.wait_recv()

    picks[...] = jnp.zeros(picks.shape, jnp.float32)
    for r in range(4):
        block = jnp.maximum(
            jnp.maximum(result_in[r], result_in[4 + r]), jnp.maximum(result_in[8 + r], result_in[12 + r])
        )
        block = jnp.maximum(block, result_in[16 + r])[:, r * cap : (r + 1) * cap]
        high = block.astype(jnp.bfloat16).astype(jnp.float32)
        middle = (block - high).astype(jnp.bfloat16).astype(jnp.float32)
        picks[r : r + 1, :] = high
        picks[4 + r : 5 + r, :] = middle
        picks[8 + r : 9 + r, :] = (block - high) - middle
    found = jnp.dot(picks[...].astype(jnp.bfloat16), at_rank, preferred_element_type=jnp.float32)
    out = jnp.zeros((1, rows), jnp.float32)
    for r in range(4):
        value = (found[r : r + 1, :] + found[4 + r : 5 + r, :]) + found[8 + r : 9 + r, :]
        out = jnp.where(owner == peer[r], value, out)
    out_ref[...] = out.reshape(rows)

    for copy in ztags + ptags + copies + [zcopies[2], zcopies[7], zcopies[8]]:
        copy.wait_send()
    for group in spreads.values():
        for copy in group:
            copy.wait_send()
    relayed(list(relays.values()), lambda copy: copy.wait_send())


def local_fused(embeddings, row_group, row_cluster):
    rows, columns = embeddings.shape
    slots = 2 * rows
    dma = pltpu.SemaphoreType.DMA
    return pl.pallas_call(
        kernel,
        out_shape=jax.ShapeDtypeStruct((rows,), jnp.float32),
        in_specs=[pl.BlockSpec(memory_space=pltpu.HBM)] * 3,
        out_specs=pl.BlockSpec(memory_space=pltpu.VMEM),
        scratch_shapes=[
            pltpu.VMEM((rows, columns), jnp.bfloat16),
            pltpu.VMEM((rows,), jnp.int32),
            pltpu.VMEM((rows,), jnp.int32),
            pltpu.VMEM((rows, columns), jnp.bfloat16),
            pltpu.VMEM((3, slots // 4, columns), jnp.bfloat16),
            pltpu.VMEM((5, slots, columns), jnp.bfloat16),
            pltpu.VMEM((4, 8, slots), jnp.float32),
            pltpu.VMEM((3, 8, slots), jnp.float32),
            pltpu.VMEM((5, 1, slots), jnp.float32),
            pltpu.VMEM((5, slots, 128), jnp.float32),
            pltpu.VMEM((5, 1, slots), jnp.float32),
            pltpu.VMEM((3, slots, 128), jnp.float32),
            pltpu.VMEM((20, 1, slots), jnp.float32),
            pltpu.VMEM((16, slots // 4), jnp.float32),
            dma((3,)),
            dma((3,)), dma((3,)), dma((9,)), dma((9,)),
            dma((4,)), dma((4,)), dma((9,)), dma((9,)),
            dma((2, 9)), dma((2, 9)), dma((9,)), dma((9,)),
            dma((20,)), dma((20,)),
        ],
        compiler_params=pltpu.CompilerParams(
            collective_id=0, has_side_effects=True, vmem_limit_bytes=64 * 1024 * 1024 - 256 * 1024
        ),
    )(embeddings, row_group, row_cluster)


def solution(mesh):
    fused = mesh.shape["grp"] == 4 and mesh.shape["tile"] == 8
    placed = (P(("grp", "tile"), None), P(("grp", "tile")), P(("grp", "tile")))
    return jax.shard_map(
        local_fused if fused else local_general,
        mesh=mesh, in_specs=placed, out_specs=P(("grp", "tile")), check_vma=False,
    )
```

```python
import jax
import jax.numpy as jnp
from jax import lax
from jax.experimental import pallas as pl
from jax.experimental.pallas import tpu as pltpu
from jax.sharding import PartitionSpec as P

MESH = pl.DeviceIdType.MESH
epsilon = 1e-06
NT = (((1,), (1,)), ((), ()))


def unit_rows(values):
    floats = values.astype(jnp.float32)
    scaled = floats * lax.rsqrt(jnp.sum(floats * floats, axis=-1, keepdims=True) + epsilon)
    return scaled.astype(jnp.bfloat16)


def slot_index(owners, groups, capacity):
    onehot = (owners[:, None] == jnp.arange(groups, dtype=jnp.int32)[None, :]).astype(jnp.int32)
    earlier = jnp.cumsum(onehot, axis=0) - onehot
    ranked = jnp.sum(earlier * onehot, axis=1)
    return owners * capacity + ranked


def masked_table(scores, left_ids, right_ids, left_pos, right_pos):
    allowed = (
        (left_ids[:, None] == right_ids[None, :])
        & (right_ids[None, :] >= 0)
        & (left_pos[:, None] != right_pos[None, :])
    )
    return jnp.where(allowed, scores, jnp.float32(-1.0))


def local_general(embeddings, row_group, row_cluster):
    row_count = embeddings.shape[0]
    columns = embeddings.shape[1]
    groups = lax.axis_size("grp")
    capacity = 2 * row_count // groups
    slots_all = groups * capacity
    placed = slot_index(row_group, groups, capacity)
    normed = unit_rows(embeddings)
    outgoing = (
        jnp.zeros((slots_all, columns), jnp.bfloat16)
        .at[placed]
        .set(normed)
        .reshape(groups, capacity, columns)
    )
    out_tags = (
        jnp.full((slots_all,), -1, jnp.int32).at[placed].set(row_cluster).reshape(groups, capacity)
    )
    members, member_ids = (
        lax.all_to_all(outgoing, "grp", split_axis=0, concat_axis=0, tiled=True),
        lax.all_to_all(out_tags, "grp", split_axis=0, concat_axis=0, tiled=True),
    )
    members = members.reshape(slots_all, columns)
    member_ids = member_ids.reshape(slots_all)
    tile_here = lax.axis_index("tile")
    local_pos = jnp.arange(slots_all, dtype=jnp.int32)
    own_pos = tile_here * slots_all + local_pos
    start_best = jnp.full((slots_all,), -1.0, jnp.float32)
    piece_rows = lax.all_gather(members, "tile", axis=0, tiled=True)
    piece_ids = lax.all_gather(member_ids, "tile", axis=0, tiled=True)
    scores = jnp.einsum("id,jd->ij", members, piece_rows, preferred_element_type=jnp.float32)
    piece_pos = jnp.arange(piece_rows.shape[0], dtype=jnp.int32)
    best_sim = jnp.maximum(
        start_best, jnp.max(masked_table(scores, member_ids, piece_ids, own_pos, piece_pos), axis=1)
    )
    results = best_sim.reshape(groups, capacity)
    arrived = lax.all_to_all(results, "grp", split_axis=0, concat_axis=0, tiled=True)
    return jnp.take(arrived.reshape(slots_all), placed)


def kernel(
    x_ref, owner_ref, cluster_ref, out_ref,
    loaded, owners, clusters, normed, send, members, tag_out, tag_in, tags, key_tags, best, key_best, result_in, picks, load_s,
    ztag_s, ztag_r, z_s, z_r, ptag_s, ptag_r, sib_s, sib_r, near_s, near_r, relay_s, relay_r, res_s, res_r,
):
    rows = x_ref.shape[0]
    groups = 4
    cap = 2 * rows // groups
    slots = groups * cap
    half = cap // 2
    early = 3 * cap
    me = lax.axis_index("grp")
    tile = lax.axis_index("tile")
    core = lax.rem(tile, 2)
    xpos = lax.rem(tile // 2, 2)
    ypos = tile // 4
    beside = 1 - 2 * core
    sib = tile + beside
    xdev = tile + 2 - 4 * xpos
    ydev = tile + 4 - 8 * ypos
    cross = 4 - xpos
    crossdev = ydev + (1 - xpos) * beside
    peer = (me, me + 1 - 2 * lax.rem(me, 2), me + 2 - 4 * (me // 2), 3 - me)

    partners = [(peer[r], tile) for r in (1, 2, 3)]
    partners += [(peer[r], device) for r in range(4) for device in (sib, xdev, ydev, ydev + beside)]
    barrier = pltpu.get_barrier_semaphore()
    for partner in partners:
        pl.semaphore_signal(barrier, inc=1, device_id=partner, device_id_type=MESH)

    loads = [
        pltpu.make_async_copy(src, dst, load_s.at[n])
        for n, (src, dst) in enumerate(((owner_ref, owners), (cluster_ref, clusters), (x_ref, loaded)))
    ]
    for load in loads:
        load.start()

    def remote(src, dst, ssem, rsem, device):
        return pltpu.make_async_remote_copy(
            src_ref=src, dst_ref=dst, send_sem=ssem, recv_sem=rsem, device_id=device, device_id_type=MESH
        )

    loads[0].wait()
    loads[1].wait()
    owner = owners[...].reshape(1, rows)
    cluster = clusters[...].reshape(1, rows)
    group_of = lax.broadcasted_iota(jnp.int32, (8, rows), 0)
    belongs = group_of == owner
    before = lax.broadcasted_iota(jnp.int32, (rows, rows), 0) < lax.broadcasted_iota(jnp.int32, (rows, rows), 1)
    earlier = jnp.dot(
        jnp.where(belongs, 1.0, 0.0).astype(jnp.bfloat16),
        jnp.where(before, 1.0, 0.0).astype(jnp.bfloat16),
        preferred_element_type=jnp.float32,
    )
    rank = jnp.sum(jnp.where(belongs, earlier, 0.0), axis=0, keepdims=True).astype(jnp.int32)
    slot = owner * cap + rank
    at_rank = jnp.where(lax.broadcasted_iota(jnp.int32, (cap, rows), 0) == rank, 1.0, 0.0).astype(jnp.bfloat16)

    loads[2].wait()
    chunk = rows // 4
    for c in range(4):
        part = pl.ds(c * chunk, chunk)
        normed[part, :] = unit_rows(loaded[part, :])

    def filled(group):
        sel = lax.broadcasted_iota(jnp.int32, (cap, rows), 0) + group * cap
        sel = jnp.where(sel == slot, 1.0, 0.0).astype(jnp.bfloat16)
        return jnp.dot(sel, normed[...], preferred_element_type=jnp.float32).astype(jnp.bfloat16)

    sixth = cap // 6
    parts = ((0, 0, 6), (1, 0, 3), (1, 3, 6), (2, 0, 1), (2, 1, 3), (2, 3, 6), (3, 0, 3), (3, 3, 6))

    def begin(part):
        r, low, high = parts[part]
        copy = remote(
            send.at[r - 1, pl.ds(low * sixth, (high - low) * sixth), :],
            members.at[0, pl.ds(r * cap + low * sixth, (high - low) * sixth), :],
            z_s.at[part], z_r.at[part], (peer[r], tile),
        )
        copy.start()
        zcopies[part] = copy

    def line_of(part):
        r, low, high = parts[part]
        return pl.ds(r * cap + low * sixth, (high - low) * sixth)

    def spread(part):
        if part:
            zcopies[part].wait_recv()
        line = line_of(part)
        src = members.at[0, line, :]
        copies = [
            remote(src, members.at[1, line, :], sib_s.at[part], sib_r.at[part], (me, sib)),
            remote(src, members.at[2, line, :], near_s.at[0, part], near_r.at[0, part], (me, xdev)),
            remote(src, members.at[3, line, :], near_s.at[1, part], near_r.at[1, part], (me, ydev)),
        ]
        for copy in copies[::-1]:
            copy.start()
        spreads[part] = copies

    def relay(part):
        spreads[part][2].wait_recv()
        line = line_of(part)
        copy = remote(members.at[3, line, :], members.at[4, line, :], relay_s.at[part], relay_r.at[part], (me, sib))

        @pl.when(xpos == 0)
        def _():
            copy.start()

        relays[part] = copy

    def relayed(copies, wait):
        @pl.when(xpos == 0)
        def _():
            for copy in copies:
                wait(copy)

    zcopies, spreads, relays = {}, {}, {}
    send[1] = filled(peer[2])
    pl.semaphore_wait(barrier, len(partners))
    begin(3)
    begin(4)
    send[0] = filled(peer[1])
    begin(1)
    members[0, 0:cap, :] = filled(me)
    spread(0)
    send[2] = filled(peer[3])

    marks = jnp.where(belongs, (cluster + 1).astype(jnp.float32), 0.0).astype(jnp.bfloat16)
    marked = lax.dot_general(marks, at_rank, NT, preferred_element_type=jnp.float32)
    tag_out[...] = jnp.zeros(tag_out.shape, jnp.float32)
    ztags = []
    for r in range(4):
        tag_out[r, :, r * cap : (r + 1) * cap] = marked
        if r:
            copy = remote(tag_out.at[r], tag_in.at[r - 1], ztag_s.at[r - 1], ztag_r.at[r - 1], (peer[r], tile))
            copy.start()
            ztags.append(copy)

    zcopies[3].wait_send()
    begin(5)
    spread(3)
    zcopies[1].wait_send()
    begin(2)
    spread(1)
    zcopies[4].wait_send()
    begin(6)
    spread(4)

    for copy in ztags:
        copy.wait_recv()
    total = tag_out[0] + tag_in[0] + tag_in[1] + tag_in[2]
    tags[0] = jnp.sum(
        jnp.where(lax.broadcasted_iota(jnp.int32, (8, slots), 0) == me, total, 0.0), axis=0, keepdims=True
    )
    ptags = []
    for n, device in enumerate((sib, xdev, ydev, ydev + beside)):
        copy = remote(tags.at[0], tags.at[1 + n], ptag_s.at[n], ptag_r.at[n], (me, device))
        copy.start()
        ptags.append(copy)

    for copy in ptags:
        copy.wait_recv()
    best[...] = jnp.full(best.shape, -1.0, jnp.float32)
    key_best[...] = jnp.full(key_best.shape, -1.0, jnp.float32)
    for n in range(5):
        for i in range(groups):
            first = i * cap // 128 * 128
            lanes = lax.broadcasted_iota(jnp.int32, (cap, 256), 1) + (first - i * cap)
            wanted = lax.broadcasted_iota(jnp.int32, (cap, 256), 0)
            picked = jnp.sum(
                jnp.where(lanes == wanted, tags[n, :, first : first + 256], 0.0), axis=1, keepdims=True
            )
            picked = jnp.where(picked > 0.0, picked, -1.0)
            key_tags[n, i * cap : (i + 1) * cap, :] = jnp.broadcast_to(picked, (cap, 128))

    def compare(kblock, keys, qblock, queries, to, own=False, back=None):
        (k0, k1), (q0, q1) = keys, queries
        shape = (k1 - k0, q1 - q0)
        scores = lax.dot_general(
            members[kblock, k0:k1, :], members[qblock, q0:q1, :], NT, preferred_element_type=jnp.float32
        )
        allowed = key_tags[kblock, k0:k1, 0:1] == tags[qblock, :, q0:q1]
        if own:
            line = lax.broadcasted_iota(jnp.int32, shape, 0) + (k0 + (kblock + qblock) * 2 * slots)
            lane = lax.broadcasted_iota(jnp.int32, shape, 1) + q0
            allowed = allowed & (line != lane)
        masked = jnp.where(allowed, scores, -1.0)
        found = jnp.max(masked, axis=0, keepdims=True)
        best[to, :, q0:q1] = jnp.maximum(best[to, :, q0:q1], found)
        if back is not None:
            full = shape[1] // 128 * 128
            across = key_best[back, k0:k1, :]
            for lane in range(0, full, 128):
                across = jnp.maximum(across, masked[:, lane : lane + 128])
            key_best[back, k0:k1, :] = across
            rest = shape[1] - full
            if rest:
                key_best[back, k0:k1, :rest] = jnp.maximum(key_best[back, k0:k1, :rest], masked[:, full:])

    first, last, whole = (0, early), (early, slots), (0, slots)

    spread(2)
    zcopies[5].wait_send()
    begin(7)
    spread(5)
    for part in range(6):
        spreads[part][0].wait_recv()

    @pl.loop(0, 2)
    def _(q):
        compare(0, first, q, first, q, own=True)

    for part in (0, 3, 1, 4, 2):
        relay(part)
    spread(6)
    relay(5)
    for part in range(6):
        spreads[part][1].wait_recv()

    def beside_block(i):
        return xpos + i * (ypos - xpos)

    @pl.loop(0, 2)
    def _(i):
        compare(2 + i, first, beside_block(i), first, beside_block(i), back=i)

    spread(7)
    relayed([relays[part] for part in range(6)], lambda copy: copy.wait_recv())

    compare(cross, first, 2, first, 2, back=2)

    relay(6)
    for part in (6, 7):
        spreads[part][0].wait_recv()

    @pl.loop(0, 2)
    def _(q):
        compare(0, first, q, last, q, own=True)

    @pl.loop(0, 2)
    def _(i):
        compare(2 + i, first, beside_block(i), last, beside_block(i), back=i)

    @pl.loop(0, 2)
    def _(q):
        compare(0, last, q, whole, q, own=True)

    relay(7)
    for part in (6, 7):
        spreads[part][1].wait_recv()

    @pl.loop(0, 2)
    def _(i):
        compare(2 + i, last, beside_block(i), whole, beside_block(i), back=i)

    def turned(back):
        return jnp.max(key_best[back].T, axis=0, keepdims=True)

    copies = []

    def give(h, device):
        for r in (3, 2, 1, 0):
            index = h * 4 + r
            if index == 0:
                result_in[0] = best[0]
                continue
            copy = remote(
                best.at[h], result_in.at[index], res_s.at[index], res_r.at[index], (peer[r], device)
            )
            copy.start()
            copies.append(copy)

    give(0, tile)
    give(1, sib)
    best[4] = turned(1)
    give(4, ydev)

    compare(cross, first, 2, last, 2, back=2)
    relayed([relays[6], relays[7]], lambda copy: copy.wait_recv())
    compare(cross, last, 2, whole, 2, back=2)

    best[3] = turned(2)
    give(3, crossdev)
    best[2] = jnp.maximum(best[2], turned(0))
    give(2, xdev)
    for copy in copies:
        copy.wait_recv()

    picks[...] = jnp.zeros(picks.shape, jnp.float32)
    for r in range(4):
        block = jnp.maximum(
            jnp.maximum(result_in[r], result_in[4 + r]), jnp.maximum(result_in[8 + r], result_in[12 + r])
        )
        block = jnp.maximum(block, result_in[16 + r])[:, r * cap : (r + 1) * cap]
        high = block.astype(jnp.bfloat16).astype(jnp.float32)
        middle = (block - high).astype(jnp.bfloat16).astype(jnp.float32)
        picks[r : r + 1, :] = high
        picks[4 + r : 5 + r, :] = middle
        picks[8 + r : 9 + r, :] = (block - high) - middle
    found = jnp.dot(picks[...].astype(jnp.bfloat16), at_rank, preferred_element_type=jnp.float32)
    out = jnp.zeros((1, rows), jnp.float32)
    for r in range(4):
        value = (found[r : r + 1, :] + found[4 + r : 5 + r, :]) + found[8 + r : 9 + r, :]
        out = jnp.where(owner == peer[r], value, out)
    out_ref[...] = out.reshape(rows)

    for copy in ztags + ptags + copies + [zcopies[2], zcopies[6], zcopies[7]]:
        copy.wait_send()
    for group in spreads.values():
        for copy in group:
            copy.wait_send()
    relayed(list(relays.values()), lambda copy: copy.wait_send())


def local_fused(embeddings, row_group, row_cluster):
    rows, columns = embeddings.shape
    slots = 2 * rows
    dma = pltpu.SemaphoreType.DMA
    return pl.pallas_call(
        kernel,
        out_shape=jax.ShapeDtypeStruct((rows,), jnp.float32),
        in_specs=[pl.BlockSpec(memory_space=pltpu.HBM)] * 3,
        out_specs=pl.BlockSpec(memory_space=pltpu.VMEM),
        scratch_shapes=[
            pltpu.VMEM((rows, columns), jnp.bfloat16),
            pltpu.VMEM((rows,), jnp.int32),
            pltpu.VMEM((rows,), jnp.int32),
            pltpu.VMEM((rows, columns), jnp.bfloat16),
            pltpu.VMEM((3, slots // 4, columns), jnp.bfloat16),
            pltpu.VMEM((5, slots, columns), jnp.bfloat16),
            pltpu.VMEM((4, 8, slots), jnp.float32),
            pltpu.VMEM((3, 8, slots), jnp.float32),
            pltpu.VMEM((5, 1, slots), jnp.float32),
            pltpu.VMEM((5, slots, 128), jnp.float32),
            pltpu.VMEM((5, 1, slots), jnp.float32),
            pltpu.VMEM((3, slots, 128), jnp.float32),
            pltpu.VMEM((20, 1, slots), jnp.float32),
            pltpu.VMEM((16, slots // 4), jnp.float32),
            dma((3,)),
            dma((3,)), dma((3,)), dma((8,)), dma((8,)),
            dma((4,)), dma((4,)), dma((8,)), dma((8,)),
            dma((2, 8)), dma((2, 8)), dma((8,)), dma((8,)),
            dma((20,)), dma((20,)),
        ],
        compiler_params=pltpu.CompilerParams(
            collective_id=0, has_side_effects=True, vmem_limit_bytes=64 * 1024 * 1024 - 256 * 1024
        ),
    )(embeddings, row_group, row_cluster)


def solution(mesh):
    fused = mesh.shape["grp"] == 4 and mesh.shape["tile"] == 8
    placed = (P(("grp", "tile"), None), P(("grp", "tile")), P(("grp", "tile")))
    return jax.shard_map(
        local_fused if fused else local_general,
        mesh=mesh, in_specs=placed, out_specs=P(("grp", "tile")), check_vma=False,
    )
```
